128 devices in a mesh: row: 16 (over z, y), col: 8 (over x, core).
Axes of the slice: x: 4, y: 4, z: 4, core: 2. Of those that a mesh axis runs over, the one named last changes fastest.
Arguments:
- tokens: bfloat16 [16384, 7168], P(('row', 'col')), may hold values from -6 to 6
- out_grad: bfloat16 [16384, 7168], P(('row', 'col')), may hold values from -3 to 3
- expert_ids: int32 [16384, 8], P(('row', 'col')), may hold values from 0 to 255, all different within a row
- route_weights: bfloat16 [16384, 8], P(('row', 'col')), may hold values from 0.049804688 to 1
- w_gate: bfloat16 [8, 7168, 2048], P('col', None, 'row'), may hold values from -0.0625 to 0.0625
- w_up: bfloat16 [8, 7168, 2048], P('col', None, 'row'), may hold values from -0.0625 to 0.0625
- w_down: bfloat16 [8, 2048, 7168], P('col', 'row'), may hold values from -0.125 to 0.125
Outputs:
- grad_tokens: bfloat16 [16384, 7168], P(('row', 'col'))
- grad_route: float32 [16384, 8], P(('row', 'col'))
- grad_gate: bfloat16 [8, 7168, 2048], P('col', None, 'row')
- grad_up: bfloat16 [8, 7168, 2048], P('col', None, 'row')
- grad_down: bfloat16 [8, 2048, 7168], P('col', 'row')
The draws below stay inside these ranges and needn't reach their ends.
All inputs are finite; a program needn't handle non-finite values.
Results may differ from the reference program's by a relative error of at most 0.029.
Values may be sent and summed in bfloat16 or wider, within the bound.
No kernel may reach another device: no remote copies, remote signals or barrier semaphores. Data moves between devices by JAX's collectives and lax.ppermute only.
A program may use at most 192 MiB of HBM per device.

```python
import math
import jax
import jax.numpy as jnp
from jax import lax

D = 7168
EXPERTS = 256
TOP = 8
HID_DEV = 128
TOK_DEV = 128
FF_EXP = 2048
EXP_WIN = 8
CAP = 6
TOKENS = 16384
N_ROW = 16
N_COL = 8


def steps_of(own_key, dims, pieces, low, high):
    gain, own = 1.0, jax.random.fold_in(own_key, 6)
    for axis_at, blocks in pieces:
        steps = jnp.exp(jax.random.uniform(jax.random.fold_in(own, axis_at), (blocks,), jnp.float32, low / len(pieces), high / len(pieces)))
        gain = gain * jnp.repeat(steps, dims[axis_at] // blocks).reshape([-1 if axis == axis_at else 1 for axis in range(len(dims))])
    return gain


def distinct(key, rows, amount, top, lift):
    ranking = jax.random.permutation(jax.random.fold_in(key, 1), amount)
    pull = ranking
    for power in range(3):
        pull = pull * pull // amount
    pull = pull * lift // amount
    tickets = jax.random.randint(jax.random.fold_in(key, 2), (rows, amount), 0, 4096) + pull
    holders = jax.random.permutation(jax.random.fold_in(key, 3), rows)[jnp.arange(amount) % rows]
    tickets = jnp.where(jnp.arange(rows)[:, None] == holders[None, :], 1 << 14, tickets)
    merit = tickets * amount + jnp.arange(amount)
    return lax.top_k(merit.astype(jnp.int32), top)[1].astype(jnp.int32)


def gaussian(stream_key, shape, spread, bound, pieces=(), kind=jnp.bfloat16):
    values = jax.random.normal(stream_key, shape, jnp.float32) * spread
    if len(pieces) > 0:
        values = steps_of(stream_key, shape, pieces, -0.22, 0.18) * values
    return jnp.clip(values, min=-bound, max=bound).astype(kind)


def setup_inputs(seed: int = 0) -> dict:
    keys = jax.random.split(jax.random.key(seed), 8)
    tokens = gaussian(keys[0], (TOKENS, D), 1.0, 6.0, ((0, 128),))
    out_grad = gaussian(keys[1], (TOKENS, D), 0.5, 3.0, ((0, 128),))
    expert_ids = distinct(keys[2], TOKENS, EXPERTS, TOP, 256)
    route_weights = jnp.clip(jnp.exp(math.log(1.0) - 2.9996462 * jax.random.uniform(keys[3], (TOKENS, TOP), jnp.float32) ** steps_of(keys[3], (TOKENS, TOP), ((0, 128),), -0.2, 0.2)), 0.049804688, 1.0).astype(jnp.bfloat16)
    w_gate = gaussian(keys[4], (EXP_WIN, D, FF_EXP), D ** -0.5, 0.0625, ((0, 8), (2, 16)))
    w_up = gaussian(keys[5], (EXP_WIN, D, FF_EXP), D ** -0.5, 0.0625, ((0, 8), (2, 16)))
    w_down = gaussian(keys[6], (EXP_WIN, FF_EXP, D), FF_EXP ** -0.5, 0.125, ((0, 8), (1, 16)))
    return {"tokens": tokens, "out_grad": out_grad, "expert_ids": expert_ids, "route_weights": route_weights, "w_gate": w_gate, "w_up": w_up, "w_down": w_down}


def place_slots(block_ids, experts_here, capacity):
    flat_ids = block_ids.reshape(-1)
    choose = (flat_ids[:, None] == jnp.arange(experts_here, dtype=jnp.int32)[None, :]).astype(jnp.int32)
    before = (jnp.cumsum(choose, axis=0) - choose).astype(jnp.int32)
    position = jnp.sum(before * choose, axis=1).astype(jnp.int32)
    kept = (flat_ids < experts_here) & (position < capacity)
    slot_ids = jnp.where(kept, flat_ids * capacity + position, -1)
    return slot_ids.reshape(block_ids.shape).astype(jnp.int32)


def pack_table(slot_ids, slot_count):
    marks = jnp.arange(slot_count, dtype=jnp.int32)
    matches = slot_ids[None, :, :] == marks[:, None, None]
    dispatch = jnp.any(matches, axis=2).astype(jnp.bfloat16)
    return dispatch, matches


def expert_backward(bundle):
    rows_x, rows_y, rows_w, gate_w, up_w, down_w = bundle
    row_total = rows_x.shape[0]
    pre_gate = jnp.dot(rows_x, gate_w, preferred_element_type=jnp.float32)
    pre_up = jnp.dot(rows_x, up_w, preferred_element_type=jnp.float32)
    sigmoid_gate = jax.nn.sigmoid(pre_gate)
    activation = pre_gate * sigmoid_gate
    hidden = (activation * pre_up).astype(jnp.bfloat16)
    raw_grad = jnp.dot(rows_y, down_w.T, preferred_element_type=jnp.float32)
    weight_col = rows_w.astype(jnp.float32)[:, None]
    hidden_grad = weight_col * raw_grad
    gate_rows = (hidden_grad * pre_up * sigmoid_gate * (1.0 + pre_gate * (1.0 - sigmoid_gate))).astype(jnp.bfloat16)
    up_rows = (hidden_grad * activation).astype(jnp.bfloat16)
    weighted = (weight_col * rows_y.astype(jnp.float32)).astype(jnp.bfloat16)
    grad_down = jnp.dot(hidden.T, weighted, preferred_element_type=jnp.float32).astype(jnp.bfloat16)
    grad_gate = jnp.dot(rows_x.T, gate_rows, preferred_element_type=jnp.float32).astype(jnp.bfloat16)
    grad_up = jnp.dot(rows_x.T, up_rows, preferred_element_type=jnp.float32).astype(jnp.bfloat16)
    block_route = jnp.sum((hidden.astype(jnp.float32) * raw_grad).reshape(row_total, N_ROW, HID_DEV), axis=2).astype(jnp.bfloat16)
    block_route = lax.optimization_barrier(block_route)
    pair_route = jnp.sum(block_route.astype(jnp.float32), axis=1).astype(jnp.bfloat16)

    def add_block(block_idx, summed):
        first_col = (block_idx * HID_DEV).astype(jnp.int32)
        gate_blk = lax.dynamic_slice_in_dim(gate_rows, first_col, HID_DEV, 1)
        up_blk = lax.dynamic_slice_in_dim(up_rows, first_col, HID_DEV, 1)
        gate_wblk = lax.dynamic_slice_in_dim(gate_w, first_col, HID_DEV, 1)
        up_wblk = lax.dynamic_slice_in_dim(up_w, first_col, HID_DEV, 1)
        partial_value = jnp.dot(gate_blk, gate_wblk.T, preferred_element_type=jnp.float32)
        partial_value = partial_value + jnp.dot(up_blk, up_wblk.T, preferred_element_type=jnp.float32)
        partial_value = lax.optimization_barrier(partial_value.astype(jnp.bfloat16))
        return summed + partial_value.astype(jnp.float32)

    pair_dx = lax.fori_loop(0, N_ROW, add_block, jnp.zeros((row_total, D), jnp.float32)).astype(jnp.bfloat16)
    return grad_gate, grad_up, grad_down, pair_dx, pair_route


def reference(tokens, out_grad, expert_ids, route_weights, w_gate, w_up, w_down):
    blocks = N_ROW * N_COL
    slot_count = EXP_WIN * CAP
    slot_ids = jax.vmap(lambda block_ids: place_slots(block_ids, EXP_WIN, CAP))(expert_ids.reshape(blocks, TOK_DEV, TOP))

    def pack_block(bundle):
        block_slots, block_x, block_y, block_w = bundle
        dispatch, matches = pack_table(block_slots, slot_count)
        packed_x = jnp.dot(dispatch, block_x, preferred_element_type=jnp.float32).astype(jnp.bfloat16)
        packed_y = jnp.dot(dispatch, block_y, preferred_element_type=jnp.float32).astype(jnp.bfloat16)
        packed_w = jnp.sum(jnp.where(matches, block_w.astype(jnp.float32)[None, :, :], jnp.float32(0.0)), axis=(1, 2)).astype(jnp.bfloat16)
        return packed_x, packed_y, packed_w

    packed_x, packed_y, packed_w = lax.map(pack_block, (slot_ids, tokens.reshape(blocks, TOK_DEV, D), out_grad.reshape(blocks, TOK_DEV, D), route_weights.reshape(blocks, TOK_DEV, TOP)))
    rows_x = packed_x.reshape(blocks, EXP_WIN, CAP, D).transpose(1, 0, 2, 3).reshape(EXP_WIN, blocks * CAP, D)
    rows_y = packed_y.reshape(blocks, EXP_WIN, CAP, D).transpose(1, 0, 2, 3).reshape(EXP_WIN, blocks * CAP, D)
    rows_w = packed_w.reshape(blocks, EXP_WIN, CAP).transpose(1, 0, 2).reshape(EXP_WIN, blocks * CAP)
    grad_gate, grad_up, grad_down, pair_dx, pair_route = lax.map(expert_backward, (rows_x, rows_y, rows_w, w_gate, w_up, w_down))
    back_dx = pair_dx.reshape(EXP_WIN, blocks, CAP, D).transpose(1, 0, 2, 3).reshape(blocks, slot_count, D)
    back_route = pair_route.reshape(EXP_WIN, blocks, CAP).transpose(1, 0, 2).reshape(blocks, slot_count)

    def unpack_block(bundle):
        block_slots, block_dx, block_route = bundle
        dispatch, matches = pack_table(block_slots, slot_count)
        token_grad = jnp.dot(dispatch.T, block_dx, preferred_element_type=jnp.float32).astype(jnp.bfloat16)
        route_grad = jnp.sum(jnp.where(matches, block_route.astype(jnp.float32)[:, None, None], jnp.float32(0.0)), axis=0)
        return token_grad, route_grad

    grad_tokens, grad_route = lax.map(unpack_block, (slot_ids, back_dx, back_route))
    return (grad_tokens.reshape(blocks * TOK_DEV, D), grad_route.reshape(blocks * TOK_DEV, TOP), grad_gate, grad_up, grad_down)
```

```python
import jax
import jax.numpy as jnp
from jax import lax
from jax.sharding import PartitionSpec as P

CAP = 6
Z = 4
Y = 4
X = 4
BF = jnp.bfloat16
F32 = jnp.float32


def shift_z(value, step):
    pairs = [(z * Y + y, (z + step) % Z * Y + y) for z in range(Z) for y in range(Y)]
    return lax.ppermute(value, "row", pairs)


def shift_y(value, step):
    pairs = [(z * Y + y, z * Y + (y + step) % Y) for z in range(Z) for y in range(Y)]
    return lax.ppermute(value, "row", pairs)


def shift_x(value, step):
    pairs = [(x * 2 + c, (x + step) % X * 2 + c) for x in range(X) for c in range(2)]
    return lax.ppermute(value, "col", pairs)


def swap_core(value):
    pairs = [(x * 2 + c, x * 2 + 1 - c) for x in range(X) for c in range(2)]
    return lax.ppermute(value, "col", pairs)


def gather_ring(block, shift):
    half = block.shape[0] // 2
    below = shift(block, 1)
    above = shift(block, -1)
    far_low = shift(below[:half], 1)
    far_high = shift(above[half:], -1)
    return jnp.concatenate([block, below, above, far_low, far_high], axis=0)


def scatter_ring(own, below, above, opposite, shift):
    half = opposite.shape[0] // 2
    far_low = shift(opposite[:half], -1)
    far_high = shift(opposite[half:], 1)
    to_below = below.at[:half].add(far_low)
    to_above = above.at[half:].add(far_high)
    return own + shift(to_below, -1) + shift(to_above, 1)


def relative_experts():
    col = lax.axis_index("col")
    x, core = col // 2, col % 2
    planes = [(x + d) % X for d in (0, 1, 2, 3)]
    return jnp.stack([2 * plane + c for c in (core, 1 - core) for plane in planes])


def place(expert_ids, route_weights):
    rel = relative_experts()
    hits = expert_ids[:, :, None] == rel[None, None, :]
    choose = jnp.any(hits, axis=1)
    tokens = expert_ids.shape[0]
    earlier = jnp.tril(jnp.ones((tokens, tokens), BF), -1)
    before = jnp.dot(earlier, choose.astype(BF), preferred_element_type=F32)
    weight = jnp.sum(jnp.where(hits, route_weights.astype(F32)[:, :, None], 0.0), axis=1)
    spot = jnp.arange(CAP, dtype=F32)
    taken = choose.T[:, None, :] & (before.T[:, None, :] == spot[None, :, None])
    dispatch = taken.reshape(8 * CAP, tokens)
    weighted = jnp.where(taken, weight.T[:, None, :], 0.0).reshape(8 * CAP, tokens)
    return hits, dispatch.astype(BF), weighted.astype(BF)


def deliver(sent):
    kept, other = sent[:24], swap_core(sent[24:])

    def rows(plane):
        return [kept[plane * 6 : plane * 6 + 6], other[plane * 6 : plane * 6 + 6]]

    to_above = jnp.concatenate(rows(1) + rows(2)[:1], axis=0)
    to_below = jnp.concatenate(rows(2)[1:] + rows(3), axis=0)
    from_below = shift_x(to_above, 1)
    from_above = shift_x(to_below, -1)
    far_low = shift_x(from_below[12:], 1)
    far_high = shift_x(from_above[:6], -1)
    return jnp.concatenate(
        rows(0) + [from_below[:12], far_low, far_high, from_above[6:]], axis=0
    )


def bring_back(rows):
    from_above = shift_x(rows[12:30], -1)
    from_below = shift_x(rows[30:48], 1)
    far_high = shift_x(from_above[12:], -1)
    far_low = shift_x(from_below[:6], 1)
    halves = [
        [rows[0:6], rows[6:12]],
        [from_above[0:6], from_above[6:12]],
        [far_high, far_low],
        [from_below[6:12], from_below[12:18]],
    ]
    kept = jnp.concatenate([h[0] for h in halves], axis=0)
    other = swap_core(jnp.concatenate([h[1] for h in halves], axis=0))
    return jnp.concatenate([kept, other], axis=0)


def turn(rows):
    slots = rows.shape[0] // 16
    return rows.reshape(4, 4, slots, -1).swapaxes(0, 1).reshape(rows.shape)


def local(tokens, out_grad, expert_ids, route_weights, w_gate, w_up, w_down):
    width = tokens.shape[1]
    hits, dispatch, weighted_dispatch = place(expert_ids, route_weights)
    send_x = jnp.dot(dispatch, tokens, preferred_element_type=F32).astype(BF)
    send_y = jnp.dot(weighted_dispatch, out_grad, preferred_element_type=F32).astype(BF)
    own = deliver(jnp.concatenate([send_x, send_y], axis=1))
    own_x, own_y = own[:, :width], own[:, width:]
    all_x = gather_ring(gather_ring(own_x, shift_z), shift_y)
    all_y = gather_ring(gather_ring(own_y, shift_y), shift_z)

    gate_up = jnp.concatenate([w_gate[0], w_up[0]], axis=1)
    hid = w_gate.shape[2]
    pre = jnp.dot(all_x, gate_up, preferred_element_type=F32)
    pre_gate, pre_up = pre[:, :hid], pre[:, hid:]
    sig = jax.nn.sigmoid(pre_gate)
    silu = pre_gate * sig
    hidden = (silu * pre_up).astype(BF)
    hidden_grad = turn(
        jnp.einsum("rd,hd->rh", all_y, w_down[0], preferred_element_type=F32)
    )
    gate_rows = (hidden_grad * pre_up * sig * (1.0 + pre_gate * (1.0 - sig))).astype(BF)
    up_rows = (hidden_grad * silu).astype(BF)
    rows = jnp.concatenate([gate_rows, up_rows], axis=1)
    route = jnp.sum(hidden.astype(F32) * hidden_grad, axis=1)

    half = width // 2
    dx_a = jnp.einsum("rh,dh->rd", rows, gate_up[:half], preferred_element_type=F32).astype(BF)
    rows_t = turn(rows)
    dx_b = jnp.einsum("rh,dh->rd", rows_t, gate_up[half:], preferred_element_type=F32).astype(BF)
    route_cols = jnp.broadcast_to(route.astype(BF)[:, None], (route.shape[0], 128))
    dx_a = jnp.concatenate([dx_a, route_cols], axis=1)

    def quarters(part):
        n = part.shape[0] // 4
        return [part[i * n : (i + 1) * n] for i in range(4)]

    own_a = scatter_ring(*quarters(scatter_ring(*quarters(dx_a), shift_y)), shift_z)
    own_b = scatter_ring(*quarters(scatter_ring(*quarters(dx_b), shift_z)), shift_y)

    grad_gu = jnp.einsum("rd,rh->dh", all_x, rows, preferred_element_type=F32).astype(BF)
    grad_down = jnp.einsum("rh,rd->hd", turn(hidden), all_y, preferred_element_type=F32)

    back = bring_back(jnp.concatenate([own_a, own_b], axis=1))
    back_dx = jnp.concatenate([back[:, :half], back[:, half + 128 :]], axis=1)
    grad_tokens = jnp.einsum("st,sd->td", dispatch, back_dx, preferred_element_type=F32)
    back_route = back[:, half].astype(F32)
    per_expert = jnp.sum(
        (dispatch.astype(F32) * back_route[:, None]).reshape(8, CAP, -1), axis=1
    )
    grad_route = jnp.sum(jnp.where(hits, per_expert.T[:, None, :], 0.0), axis=2)
    grad_route = grad_route / route_weights.astype(F32)
    return (
        grad_tokens.astype(BF),
        grad_route,
        grad_gu[None, :, :hid],
        grad_gu[None, :, hid:],
        grad_down.astype(BF)[None],
    )


def solution(mesh):
    both = P(("row", "col"), None)
    columns = P("col", None, "row")
    rows = P("col", "row", None)
    return jax.shard_map(
        local,
        mesh=mesh,
        in_specs=(both, both, both, both, columns, columns, rows),
        out_specs=(both, both, columns, columns, rows),
        check_vma=False,
    )
```

```python
import jax
import jax.numpy as jnp
from jax import lax
from jax.experimental import pallas as pl
from jax.experimental.pallas import tpu as pltpu
from jax.sharding import PartitionSpec as P

CAP = 6
Z = 4
Y = 4
X = 4
BF = jnp.bfloat16
F32 = jnp.float32
OFFSETS = (0, -1, 1, 2)
VMEM = 40 * 2**20
SLOTS = 8


def shift_z(value, step):
    pairs = [(z * Y + y, (z + step) % Z * Y + y) for z in range(Z) for y in range(Y)]
    return lax.ppermute(value, "row", pairs)


def shift_y(value, step):
    pairs = [(z * Y + y, z * Y + (y + step) % Y) for z in range(Z) for y in range(Y)]
    return lax.ppermute(value, "row", pairs)


def gather_ring(block, shift):
    half = block.shape[0] // 2
    below = shift(block, 1)
    above = shift(block, -1)
    far_low = shift(below[:half], 1)
    far_high = shift(above[half:], -1)
    return [block, below, above, far_low, far_high]


def gather_direct(block, shift):
    return [block, shift(block, 1), shift(block, -1), shift(block, 2)]


def exchange(blocks, shift):
    return [
        blocks[0],
        shift(blocks[2], 1),
        shift(blocks[1], -1),
        shift(blocks[3], 2),
    ]


def seen_from(rows, offset, axis):
    order = [OFFSETS.index((o - offset + 1) % 4 - 1) for o in OFFSETS]
    return jnp.concatenate(
        [lax.slice_in_dim(rows, k, k + 1, axis=axis) for k in order], axis=axis
    )


def dx_part(rows, weights, shift):
    blocks = gather_direct(rows, shift)
    blocks = [seen_from(b, o, 1) for b, o in zip(blocks, OFFSETS)]
    wide = jnp.concatenate(blocks, axis=3)
    wide = wide.reshape(-1, wide.shape[3])
    return jnp.einsum("rh,dh->rd", wide, weights, preferred_element_type=F32).astype(BF)


def sum_over(part, shift):
    n = part.shape[0] // 4
    pieces = exchange([part[i * n : (i + 1) * n] for i in range(4)], shift)
    return sum(p.astype(F32) for p in pieces).astype(BF)


def spread(part, shift):
    n = part.shape[0] // 4
    return exchange([part[i * n : (i + 1) * n] for i in range(4)], shift)


def relative_experts():
    col = lax.axis_index("col")
    x, core = col // 2, col % 2
    planes = [(x + d) % X for d in range(4)]
    return jnp.stack([2 * plane + c for plane in planes for c in (core, 1 - core)])


def shift_x(value, step):
    pairs = [(x * 2 + c, (x + step) % X * 2 + c) for x in range(X) for c in range(2)]
    return lax.ppermute(value, "col", pairs)


def swap_core(value):
    pairs = [(x * 2 + c, x * 2 + 1 - c) for x in range(X) for c in range(2)]
    return lax.ppermute(value, "col", pairs)


def pack_kernel(rel, ids, weights, tokens, grads, *outs):
    pieces, table_out, table, weighted = outs[:4], outs[4], outs[5], outs[6]

    @pl.when(pl.program_id(0) == 0)
    def _():
        n = ids.shape[1]
        expert = lax.broadcasted_iota(jnp.int32, (8, n), 0)
        route = weights[...].astype(F32)
        choose = jnp.zeros((8, n), F32)
        weight = jnp.zeros((8, n), F32)
        for e in range(8):
            hit = ids[...] == rel[e]
            any_hit = jnp.max(jnp.where(hit, 1.0, 0.0), axis=0, keepdims=True)
            total = jnp.sum(jnp.where(hit, route, 0.0), axis=0, keepdims=True)
            choose = jnp.where(expert == e, any_hit, choose)
            weight = jnp.where(expert == e, total, weight)
        earlier = lax.broadcasted_iota(jnp.int32, (n, n), 0) < lax.broadcasted_iota(
            jnp.int32, (n, n), 1
        )
        before = jnp.dot(
            choose.astype(BF), jnp.where(earlier, 1.0, 0.0).astype(BF),
            preferred_element_type=F32,
        )
        spot = jnp.where(choose > 0.0, before, float(CAP))
        spot = jnp.broadcast_to(spot[:, None, :], (8, SLOTS, n))
        row = lax.broadcasted_iota(jnp.int32, (8, SLOTS, n), 1).astype(F32)
        taken = jnp.where((spot == row) & (row < float(CAP)), 1.0, 0.0)
        scaled = taken * jnp.broadcast_to(weight[:, None, :], (8, SLOTS, n))
        table[...] = taken.reshape(8 * SLOTS, n).astype(BF)
        weighted[...] = scaled.reshape(8 * SLOTS, n).astype(BF)
        table_out[...] = table[...]

    x = jnp.dot(table[...], tokens[...], preferred_element_type=F32)
    y = jnp.dot(weighted[...], grads[...], preferred_element_type=F32)
    for e in range(8):
        rows = slice(e * SLOTS, e * SLOTS + CAP)
        pieces[e // 2][e % 2, 0] = x[rows].astype(BF)
        pieces[e // 2][e % 2, 1] = y[rows].astype(BF)


def pack(rel, ids, weights, tokens, grads, steps=2):
    n, width = tokens.shape
    block = width // steps
    whole = lambda i, rel: (0, 0)
    column = lambda i, rel: (0, i)
    return pl.pallas_call(
        pack_kernel,
        grid_spec=pltpu.PrefetchScalarGridSpec(
            num_scalar_prefetch=1,
            grid=(steps,),
            in_specs=[
                pl.BlockSpec((8, n), whole),
                pl.BlockSpec((8, n), whole),
                pl.BlockSpec((n, block), column),
                pl.BlockSpec((n, block), column),
            ],
            out_specs=[pl.BlockSpec((2, 2, CAP, block), lambda i, rel: (0, 0, 0, i))] * 4
            + [pl.BlockSpec((8 * SLOTS, n), whole)],
            scratch_shapes=[pltpu.VMEM((8 * SLOTS, n), BF), pltpu.VMEM((8 * SLOTS, n), BF)],
        ),
        out_shape=[jax.ShapeDtypeStruct((2, 2, CAP, width), BF)] * 4
        + [jax.ShapeDtypeStruct((8 * SLOTS, n), BF)],
        cost_estimate=pl.CostEstimate(
            flops=4 * 64 * n * width, bytes_accessed=6 * n * width, transcendentals=0
        ),
        compiler_params=pltpu.CompilerParams(vmem_limit_bytes=60 * 2**20),
    )(rel, ids, weights, tokens, grads)


def spread_table(rows, columns):
    padded, packed = (0, 1) if rows > columns else (1, 0)
    a = lax.broadcasted_iota(jnp.int32, (rows, columns), padded)
    b = lax.broadcasted_iota(jnp.int32, (rows, columns), packed)
    hit = (a % SLOTS < CAP) & (a // SLOTS * CAP + a % SLOTS == b)
    return jnp.where(hit, 1.0, 0.0).astype(BF)


def assemble_kernel(*refs):
    planes, swapped, own_x, own_y, padded = refs[:4], refs[4], refs[5], refs[6], refs[7]
    table = spread_table(8 * CAP, 8 * SLOTS)
    padded[...] = jnp.zeros_like(padded)
    for which, out in ((0, own_x), (1, own_y)):
        for e in range(8):
            rows = planes[e // 2][0, which] if e % 2 == 0 else swapped[e // 2, which]
            padded[e * SLOTS : e * SLOTS + CAP] = rows.astype(F32)
        out[...] = jnp.dot(
            table, padded[...].astype(BF), preferred_element_type=F32
        ).astype(BF)


def assemble(planes, swapped, steps=2):
    width = swapped.shape[3]
    block = width // steps
    first = lambda i: (0, 0, 0, i)
    return pl.pallas_call(
        assemble_kernel,
        grid=(steps,),
        in_specs=[pl.BlockSpec((1, 2, CAP, block), first)] * 4
        + [pl.BlockSpec((4, 2, CAP, block), first)],
        out_specs=[pl.BlockSpec((8 * CAP, block), lambda i: (0, i))] * 2,
        scratch_shapes=[pltpu.VMEM((8 * SLOTS, block), F32)],
        out_shape=[jax.ShapeDtypeStruct((8 * CAP, width), BF)] * 2,
        cost_estimate=pl.CostEstimate(
            flops=4 * 64 * 48 * width, bytes_accessed=8 * 48 * width, transcendentals=0
        ),
        compiler_params=pltpu.CompilerParams(vmem_limit_bytes=VMEM),
    )(*planes, swapped)


def regroup_kernel(*refs):
    own, outs = refs[:8], refs[8:]
    size = own[4].shape[1]
    table = spread_table(8 * SLOTS, 8 * CAP)

    def put(rows, start):
        wide = jnp.dot(table, rows, preferred_element_type=F32)
        for e in range(8):
            outs[e // 2][e % 2, :, start : start + rows.shape[1]] = wide[
                e * SLOTS : e * SLOTS + CAP
            ].astype(BF)

    for j in range(8):
        put(own[j][:, :size], j * size)
    route = sum(own[j][:, size:].astype(F32) for j in range(4))
    put(route.astype(BF), 8 * size)


def regroup(own_a, own_b):
    width = 8 * own_b[0].shape[1]
    return pl.pallas_call(
        regroup_kernel,
        out_shape=[jax.ShapeDtypeStruct((2, CAP, width + 128), BF)] * 4,
        cost_estimate=pl.CostEstimate(
            flops=2 * 64 * 48 * width, bytes_accessed=4 * 48 * width, transcendentals=0
        ),
        compiler_params=pltpu.CompilerParams(vmem_limit_bytes=VMEM),
    )(*own_a, *own_b)


def unpack_kernel(scalars, ids, weights, table, *refs):
    planes, swapped, grads, route_out, padded = refs[:4], refs[4], refs[5], refs[6], refs[7]
    n, width = ids.shape[1], grads.shape[1]
    size = width // 8
    padded[...] = jnp.zeros_like(padded)

    def load(start, columns):
        for e in range(8):
            part = (slice(None), pl.ds(start, columns))
            rows = planes[e // 2].at[0][part] if e % 2 == 0 else swapped.at[e // 2][part]
            padded[e * SLOTS : e * SLOTS + CAP, :columns] = rows.astype(F32)

    load(width, 128)
    per_slot = table[...].astype(F32) * padded[:, :1]
    per_expert = jnp.sum(per_slot.reshape(8, SLOTS, n), axis=1)
    total = jnp.zeros((8, n), F32)
    for e in range(8):
        total = total + jnp.where(ids[...] == scalars[e], per_expert[e : e + 1], 0.0)
    route_out[...] = total / weights[...].astype(F32)
    for j in range(8):
        load(j * size, size)
        at = (j + scalars[8]) % 4 if j < 4 else 4 + (j + scalars[9]) % 4
        grads[:, pl.ds(pl.multiple_of(at * size, 128), size)] = lax.dot_general(
            table[...], padded[...].astype(BF), (((0,), (0,)), ((), ())),
            preferred_element_type=F32,
        ).astype(BF)


def unpack(scalars, ids, weights, table, planes, swapped):
    n, width = ids.shape[1], swapped.shape[2] - 128
    whole = lambda i, s: (0, 0)
    first = lambda i, s: (0, 0, 0)
    return pl.pallas_call(
        unpack_kernel,
        grid_spec=pltpu.PrefetchScalarGridSpec(
            num_scalar_prefetch=1,
            grid=(1,),
            in_specs=[
                pl.BlockSpec((8, n), whole),
                pl.BlockSpec((8, n), whole),
                pl.BlockSpec((8 * SLOTS, n), whole),
            ]
            + [pl.BlockSpec((1, CAP, width + 128), first)] * 4
            + [pl.BlockSpec((4, CAP, width + 128), first)],
            out_specs=[pl.BlockSpec((n, width), whole), pl.BlockSpec((8, n), whole)],
            scratch_shapes=[pltpu.VMEM((8 * SLOTS, width // 8), F32)],
        ),
        out_shape=[
            jax.ShapeDtypeStruct((n, width), BF),
            jax.ShapeDtypeStruct((8, n), F32),
        ],
        cost_estimate=pl.CostEstimate(
            flops=2 * 64 * n * width, bytes_accessed=4 * n * width, transcendentals=0
        ),
        compiler_params=pltpu.CompilerParams(vmem_limit_bytes=VMEM),
    )(scalars, ids, weights, table, *planes, swapped)


def grads_kernel(*refs):
    xs, ys, rows, hidden, gate, up, down = refs[:5], refs[5:10], *refs[10:]
    sum_gu = sum_down = start = 0
    for x, y in zip(xs, ys):
        part = slice(start, start + x.shape[0])
        start = start + x.shape[0]
        sum_gu = sum_gu + lax.dot_general(
            x[...], rows[part], (((0,), (0,)), ((), ())), preferred_element_type=F32
        )
        sum_down = sum_down + lax.dot_general(
            hidden[part], y[...], (((0,), (0,)), ((), ())), preferred_element_type=F32
        )
    hid = gate.shape[1]
    gate[...] = sum_gu[:, :hid].astype(BF)
    up[...] = sum_gu[:, hid:].astype(BF)
    down[...] = sum_down.astype(BF)


def weight_grads(xs, ys, rows, hidden, steps=8):
    width, total, hid = xs[0].shape[1], rows.shape[0], hidden.shape[1]
    block = width // steps
    column = lambda i: (0, i)
    return pl.pallas_call(
        grads_kernel,
        grid=(steps,),
        in_specs=[pl.BlockSpec((p.shape[0], block), column) for p in (*xs, *ys)]
        + [pl.BlockSpec((total, 2 * hid), lambda i: (0, 0))]
        + [pl.BlockSpec((total, hid), lambda i: (0, 0))],
        out_specs=[pl.BlockSpec((block, hid), lambda i: (i, 0))] * 2
        + [pl.BlockSpec((hid, block), column)],
        out_shape=[jax.ShapeDtypeStruct((width, hid), BF)] * 2
        + [jax.ShapeDtypeStruct((hid, width), BF)],
        cost_estimate=pl.CostEstimate(
            flops=6 * total * hid * width,
            bytes_accessed=4 * total * width + 6 * hid * width,
            transcendentals=0,
        ),
        compiler_params=pltpu.CompilerParams(vmem_limit_bytes=VMEM),
    )(*xs, *ys, rows, hidden)


def join_kernel(place, *refs):
    for i in range(8):
        refs[16 + i][:, :128] = refs[i][...]
        refs[16 + i][:, 128:] = refs[8 + i][...]


def join_weights(place, gate, up):
    depth, hid = gate.shape
    size = depth // 8

    def block(i):
        half, at = (0, 0) if i < 4 else (4, 1)
        return pl.BlockSpec((size, hid), lambda g, p: (half + (p[at] + i) % 4, 0))

    return pl.pallas_call(
        join_kernel,
        grid_spec=pltpu.PrefetchScalarGridSpec(
            num_scalar_prefetch=1,
            grid=(1,),
            in_specs=[block(i) for i in range(8)] * 2,
            out_specs=[pl.BlockSpec((size, 2 * hid), lambda g, p: (0, 0))] * 8,
        ),
        out_shape=[jax.ShapeDtypeStruct((size, 2 * hid), BF)] * 8,
        cost_estimate=pl.CostEstimate(
            flops=0, bytes_accessed=8 * depth * hid, transcendentals=0
        ),
    )(place, *[gate] * 8, *[up] * 8)


def turn(rows):
    slots = rows.shape[0] // 16
    return rows.reshape(4, 4, slots, -1).swapaxes(0, 1).reshape(rows.shape)


def local(tokens, out_grad, expert_ids, route_weights, w_gate, w_up, w_down):
    width, hid = tokens.shape[1], w_gate.shape[2]
    z, y = lax.axis_index("row") // Y, lax.axis_index("row") % Y
    rel = relative_experts().astype(jnp.int32)
    ids, route_w = expert_ids.T, route_weights.T
    *planes, table = pack(rel, ids, route_w, tokens, out_grad)
    planes = planes[:1] + [shift_x(p, d + 1) for d, p in enumerate(planes[1:])]
    blocks = join_weights(jnp.stack([z, y]).astype(jnp.int32), w_gate[0], w_up[0])
    own_a, next_a, far_a, last_a, own_b, next_b, far_b, last_b = blocks
    below_a, above_a = shift_z(next_a, 1), shift_z(last_a, -1)
    planes, below_a, above_a, far_a, next_b, far_b, last_b = lax.optimization_barrier(
        (planes, below_a, above_a, far_a, next_b, far_b, last_b)
    )
    far_a = shift_z(far_a, 2)
    below_b, above_b, far_b = shift_y(next_b, 1), shift_y(last_b, -1), shift_y(far_b, 2)
    gate_up = jnp.concatenate([w_gate[0], w_up[0]], axis=1)
    size = width // 8
    own_x, own_y = assemble(planes, swap_core(jnp.stack([p[1] for p in planes])))
    own_x, own_y, far_a, below_b, above_b, far_b = lax.optimization_barrier(
        (own_x, own_y, far_a, below_b, above_b, far_b)
    )
    weights_a = jnp.concatenate([own_a, below_a, above_a, far_a], axis=1)
    weights_b = jnp.concatenate([own_b, below_b, above_b, far_b], axis=1)
    ring_x = jnp.concatenate(gather_ring(own_x, shift_z), axis=0)
    ring_y = jnp.concatenate(gather_ring(own_y, shift_y), axis=0)
    parts_x = gather_ring(ring_x, shift_y)
    parts_y = gather_ring(ring_y, shift_z)

    pre = jnp.concatenate(
        [jnp.dot(p, gate_up, preferred_element_type=F32) for p in parts_x], axis=0
    )
    pre_gate, pre_up = pre[:, :hid], pre[:, hid:]
    sig = jax.nn.sigmoid(pre_gate)
    silu = pre_gate * sig
    hidden = (silu * pre_up).astype(BF)
    hidden_grad = turn(
        jnp.concatenate(
            [
                jnp.einsum("rd,hd->rh", p, w_down[0], preferred_element_type=F32)
                for p in parts_y
            ],
            axis=0,
        )
    )
    gate_rows = (hidden_grad * pre_up * sig * (1.0 + pre_gate * (1.0 - sig))).astype(BF)
    up_rows = (hidden_grad * silu).astype(BF)
    rows = jnp.concatenate([gate_rows, up_rows], axis=1)
    route = jnp.sum(hidden.astype(F32) * hidden_grad, axis=1)

    slots = rows.shape[0] // 16
    route_cols = jnp.broadcast_to(route.astype(BF)[:, None], (route.shape[0], 128))
    dx_a = dx_part(rows.reshape(4, 4, slots, -1), weights_a, shift_z)
    dx_b = dx_part(turn(rows).reshape(4, 4, slots, -1), weights_b, shift_y)
    dx_a, dx_b, rows, hidden = lax.optimization_barrier((dx_a, dx_b, rows, hidden))
    sum_a = sum_over(jnp.concatenate([dx_a, route_cols], axis=1), shift_y)
    sum_b = sum_over(dx_b, shift_z)
    grads = weight_grads(parts_x, parts_y, rows, turn(hidden))
    sum_a, sum_b, grads = lax.optimization_barrier((sum_a, sum_b, grads))
    own_a = spread(sum_a, shift_z)
    own_b = spread(sum_b, shift_y)
    order = (0, 2, 3, 1)
    to_send = list(regroup([own_a[k] for k in order], [own_b[k] for k in order]))
    back = to_send[:1] + [shift_x(p, -d - 1) for d, p in enumerate(to_send[1:])]
    swapped = swap_core(jnp.stack([p[1] for p in back]))
    scalars = jnp.concatenate([rel, jnp.stack([z, y]).astype(jnp.int32)])
    grad_tokens, grad_route = unpack(scalars, ids, route_w, table, back, swapped)
    return (
        grad_tokens,
        grad_route.T,
        grads[0][None],
        grads[1][None],
        grads[2][None],
    )


def solution(mesh):
    both = P(("row", "col"), None)
    columns = P("col", None, "row")
    rows = P("col", "row", None)
    return jax.shard_map(
        local,
        mesh=mesh,
        in_specs=(both, both, both, both, columns, columns, rows),
        out_specs=(both, both, columns, columns, rows),
        check_vma=False,
    )
```

```python
import jax
import jax.numpy as jnp
from jax import lax
from jax.experimental import pallas as pl
from jax.experimental.pallas import tpu as pltpu
from jax.sharding import PartitionSpec as P

CAP = 6
Z = 4
Y = 4
X = 4
BF = jnp.bfloat16
F32 = jnp.float32
OFFSETS = (0, -1, 1, 2)
VMEM = 40 * 2**20
SLOTS = 8


def shift_z(value, step):
    pairs = [(z * Y + y, (z + step) % Z * Y + y) for z in range(Z) for y in range(Y)]
    return lax.ppermute(value, "row", pairs)


def shift_y(value, step):
    pairs = [(z * Y + y, z * Y + (y + step) % Y) for z in range(Z) for y in range(Y)]
    return lax.ppermute(value, "row", pairs)


def gather_ring(block, shift):
    half = block.shape[0] // 2
    below = shift(block, 1)
    above = shift(block, -1)
    far_low = shift(below[:half], 1)
    far_high = shift(above[half:], -1)
    return [block, below, above, far_low, far_high]


def gather_direct(block, shift):
    return [block, shift(block, 1), shift(block, -1), shift(block, 2)]


def exchange(blocks, shift):
    return [
        blocks[0],
        shift(blocks[2], 1),
        shift(blocks[1], -1),
        shift(blocks[3], 2),
    ]


def seen_from(rows, offset, axis):
    order = [OFFSETS.index((o - offset + 1) % 4 - 1) for o in OFFSETS]
    return jnp.concatenate(
        [lax.slice_in_dim(rows, k, k + 1, axis=axis) for k in order], axis=axis
    )


def dx_part(rows, weights, shift):
    blocks = gather_direct(rows, shift)
    blocks = [seen_from(b, o, 1) for b, o in zip(blocks, OFFSETS)]
    wide = jnp.concatenate(blocks, axis=3)
    wide = wide.reshape(-1, wide.shape[3])
    return jnp.einsum("rh,dh->rd", wide, weights, preferred_element_type=F32).astype(BF)


def sum_over(part, shift):
    n = part.shape[0] // 4
    pieces = exchange([part[i * n : (i + 1) * n] for i in range(4)], shift)
    return sum(p.astype(F32) for p in pieces).astype(BF)


def spread(part, shift):
    n = part.shape[0] // 4
    return exchange([part[i * n : (i + 1) * n] for i in range(4)], shift)


def relative_experts():
    col = lax.axis_index("col")
    x, core = col // 2, col % 2
    planes = [(x + d) % X for d in range(4)]
    return jnp.stack([2 * plane + c for plane in planes for c in (core, 1 - core)])


def shift_x(value, step):
    pairs = [(x * 2 + c, (x + step) % X * 2 + c) for x in range(X) for c in range(2)]
    return lax.ppermute(value, "col", pairs)


def swap_core(value):
    pairs = [(x * 2 + c, x * 2 + 1 - c) for x in range(X) for c in range(2)]
    return lax.ppermute(value, "col", pairs)


def pack_kernel(rel, ids, weights, tokens, grads, *outs):
    pieces, table_out, table_x, table_y = outs[:4], outs[4], outs[5], outs[6]

    @pl.when(pl.program_id(0) == 0)
    def _():
        n = ids.shape[1]
        expert = lax.broadcasted_iota(jnp.int32, (8, n), 0)
        route = weights[...].astype(F32)
        choose = jnp.zeros((8, n), F32)
        weight = jnp.zeros((8, n), F32)
        for e in range(8):
            hit = ids[...] == rel[e]
            any_hit = jnp.max(jnp.where(hit, 1.0, 0.0), axis=0, keepdims=True)
            total = jnp.sum(jnp.where(hit, route, 0.0), axis=0, keepdims=True)
            choose = jnp.where(expert == e, any_hit, choose)
            weight = jnp.where(expert == e, total, weight)
        earlier = lax.broadcasted_iota(jnp.int32, (n, n), 0) < lax.broadcasted_iota(
            jnp.int32, (n, n), 1
        )
        before = jnp.dot(
            choose.astype(BF), jnp.where(earlier, 1.0, 0.0).astype(BF),
            preferred_element_type=F32,
        )
        spot = jnp.where(choose > 0.0, before, float(CAP))
        spot = jnp.broadcast_to(spot[:, None, :], (8, SLOTS, n))
        row = lax.broadcasted_iota(jnp.int32, (8, SLOTS, n), 1).astype(F32)
        taken = jnp.where((spot == row) & (row < float(CAP)), 1.0, 0.0)
        scaled = taken * jnp.broadcast_to(weight[:, None, :], (8, SLOTS, n))
        taken = taken.reshape(8 * SLOTS, n).astype(BF)
        scaled = scaled.reshape(8 * SLOTS, n).astype(BF)
        table_out[...] = taken
        row = lax.broadcasted_iota(jnp.int32, (96, 8 * SLOTS), 0)
        pad = lax.broadcasted_iota(jnp.int32, (96, 8 * SLOTS), 1)
        same = (row // 12 == pad // SLOTS) & (row % CAP == pad % SLOTS)
        for which, source, out in ((0, taken, table_x), (1, scaled, table_y)):
            pick = jnp.where(same & (row // CAP % 2 == which), 1.0, 0.0).astype(BF)
            out[...] = jnp.dot(pick, source, preferred_element_type=F32).astype(BF)

    rows = jnp.dot(table_x[...], tokens[...], preferred_element_type=F32)
    rows = rows + jnp.dot(table_y[...], grads[...], preferred_element_type=F32)
    for plane in range(4):
        pieces[plane][...] = rows[plane * 24 : plane * 24 + 24].astype(BF)


def pack(rel, ids, weights, tokens, grads, steps=2):
    n, width = tokens.shape
    block = width // steps
    whole = lambda i, rel: (0, 0)
    column = lambda i, rel: (0, i)
    return pl.pallas_call(
        pack_kernel,
        grid_spec=pltpu.PrefetchScalarGridSpec(
            num_scalar_prefetch=1,
            grid=(steps,),
            in_specs=[
                pl.BlockSpec((8, n), whole),
                pl.BlockSpec((8, n), whole),
                pl.BlockSpec((n, block), column),
                pl.BlockSpec((n, block), column),
            ],
            out_specs=[pl.BlockSpec((24, block), column)] * 4
            + [pl.BlockSpec((8 * SLOTS, n), whole)],
            scratch_shapes=[pltpu.VMEM((96, n), BF), pltpu.VMEM((96, n), BF)],
        ),
        out_shape=[jax.ShapeDtypeStruct((24, width), BF)] * 4
        + [jax.ShapeDtypeStruct((8 * SLOTS, n), BF)],
        cost_estimate=pl.CostEstimate(
            flops=4 * 64 * n * width, bytes_accessed=6 * n * width, transcendentals=0
        ),
        compiler_params=pltpu.CompilerParams(vmem_limit_bytes=60 * 2**20),
    )(rel, ids, weights, tokens, grads)


def other_core_kernel(*refs):
    planes, out, held = refs[:4], refs[4], refs[5]
    for plane in range(4):
        held[plane * 24 : plane * 24 + 24] = planes[plane][...].astype(F32)
    row = lax.broadcasted_iota(jnp.int32, (48, 96), 0)
    source = lax.broadcasted_iota(jnp.int32, (48, 96), 1)
    pick = jnp.where(row // 12 * 24 + 12 + row % 12 == source, 1.0, 0.0).astype(BF)
    out[...] = jnp.dot(pick, held[...].astype(BF), preferred_element_type=F32).astype(BF)


def other_core(planes, steps=2):
    width = planes[0].shape[1]
    block = width // steps
    column = lambda i: (0, i)
    return pl.pallas_call(
        other_core_kernel,
        grid=(steps,),
        in_specs=[pl.BlockSpec((24, block), column)] * 4,
        out_specs=pl.BlockSpec((48, block), column),
        scratch_shapes=[pltpu.VMEM((96, block), F32)],
        out_shape=jax.ShapeDtypeStruct((48, width), BF),
        cost_estimate=pl.CostEstimate(
            flops=2 * 48 * 96 * width, bytes_accessed=300 * width, transcendentals=0
        ),
        compiler_params=pltpu.CompilerParams(vmem_limit_bytes=VMEM),
    )(*planes)


def assemble_kernel(*refs):
    planes, swapped, own_x, own_y, held = refs[:4], refs[4], refs[5], refs[6], refs[7]
    for plane in range(4):
        held[plane * 24 : plane * 24 + 24] = planes[plane][...].astype(F32)
    held[96:] = swapped[...].astype(F32)
    rows = held[...].astype(BF)
    row = lax.broadcasted_iota(jnp.int32, (48, 144), 0)
    source = lax.broadcasted_iota(jnp.int32, (48, 144), 1)
    plane, flip, slot = row // 12, row // CAP % 2, row % CAP
    start = jnp.where(flip == 0, plane * 24, 96 + plane * 12) + slot
    for which, out in ((0, own_x), (1, own_y)):
        pick = jnp.where(start + which * CAP == source, 1.0, 0.0).astype(BF)
        out[...] = jnp.dot(pick, rows, preferred_element_type=F32).astype(BF)


def assemble(planes, swapped, steps=2):
    width = swapped.shape[1]
    block = width // steps
    column = lambda i: (0, i)
    return pl.pallas_call(
        assemble_kernel,
        grid=(steps,),
        in_specs=[pl.BlockSpec((24, block), column)] * 4 + [pl.BlockSpec((48, block), column)],
        out_specs=[pl.BlockSpec((8 * CAP, block), column)] * 2,
        scratch_shapes=[pltpu.VMEM((144, block), F32)],
        out_shape=[jax.ShapeDtypeStruct((8 * CAP, width), BF)] * 2,
        cost_estimate=pl.CostEstimate(
            flops=4 * 144 * 48 * width, bytes_accessed=500 * width, transcendentals=0
        ),
        compiler_params=pltpu.CompilerParams(vmem_limit_bytes=VMEM),
    )(*planes, swapped)


def regroup_kernel(*refs):
    own, outs, held = refs[:8], refs[8:12], refs[12]
    size = own[4].shape[1]
    for j in range(8):
        held[:, j * size : (j + 1) * size] = own[j][:, :size]
    route = sum(own[j][:, size:].astype(F32) for j in range(4)).astype(BF)
    held[:, 8 * size : 8 * size + 128] = route
    held[:, 8 * size + 128 :] = route
    half = outs[0].shape[1]
    row = lax.broadcasted_iota(jnp.int32, (96, 8 * CAP), 0)
    source = lax.broadcasted_iota(jnp.int32, (96, 8 * CAP), 1)
    total = 0.0
    for which in range(2):
        pick = (row // 12 * CAP + row % CAP == source) & (row // CAP % 2 == which)
        total = total + jnp.dot(
            jnp.where(pick, 1.0, 0.0).astype(BF),
            held[:, which * half : (which + 1) * half],
            preferred_element_type=F32,
        )
    for plane in range(4):
        outs[plane][...] = total[plane * 24 : plane * 24 + 24].astype(BF)


def regroup(own_a, own_b):
    width = 8 * own_b[0].shape[1] + 256
    return pl.pallas_call(
        regroup_kernel,
        out_shape=[jax.ShapeDtypeStruct((24, width // 2), BF)] * 4,
        scratch_shapes=[pltpu.VMEM((8 * CAP, width), BF)],
        cost_estimate=pl.CostEstimate(
            flops=4 * 96 * 48 * width, bytes_accessed=4 * 48 * width, transcendentals=0
        ),
        compiler_params=pltpu.CompilerParams(vmem_limit_bytes=VMEM),
    )(*own_a, *own_b)


def unpack_kernel(scalars, ids, weights, table, *refs):
    planes, swapped, grads, route_out, held, padded = refs[:4], refs[4], *refs[5:]
    n, width = ids.shape[1], grads.shape[1]
    size, half = width // 8, swapped.shape[1]
    for plane in range(4):
        held[plane * 24 : plane * 24 + 24] = planes[plane][...].astype(F32)
    held[96:] = swapped[...].astype(F32)
    rows = held[...].astype(BF)
    row = lax.broadcasted_iota(jnp.int32, (8 * SLOTS, 144), 0)
    source = lax.broadcasted_iota(jnp.int32, (8 * SLOTS, 144), 1)
    plane, flip, slot = row // 16, row // SLOTS % 2, row % SLOTS
    start = jnp.where(flip == 0, plane * 24, 96 + plane * 12) + slot
    for which in range(2):
        pick = (start + which * CAP == source) & (slot < CAP)
        padded[:, which * half : (which + 1) * half] = jnp.dot(
            jnp.where(pick, 1.0, 0.0).astype(BF), rows, preferred_element_type=F32
        ).astype(BF)

    per_slot = table[...].astype(F32) * padded[:, width : width + 1].astype(F32)
    per_expert = jnp.sum(per_slot.reshape(8, SLOTS, n), axis=1)
    total = jnp.zeros((8, n), F32)
    for e in range(8):
        total = total + jnp.where(ids[...] == scalars[e], per_expert[e : e + 1], 0.0)
    route_out[...] = total / weights[...].astype(F32)
    for j in range(8):
        at = (j + scalars[8]) % 4 if j < 4 else 4 + (j + scalars[9]) % 4
        grads[:, pl.ds(pl.multiple_of(at * size, 128), size)] = lax.dot_general(
            table[...], padded[:, j * size : (j + 1) * size], (((0,), (0,)), ((), ())),
            preferred_element_type=F32,
        ).astype(BF)


def unpack(scalars, ids, weights, table, planes, swapped):
    n, half = ids.shape[1], swapped.shape[1]
    width = 2 * half - 256
    whole = lambda i, s: (0, 0)
    return pl.pallas_call(
        unpack_kernel,
        grid_spec=pltpu.PrefetchScalarGridSpec(
            num_scalar_prefetch=1,
            grid=(1,),
            in_specs=[
                pl.BlockSpec((8, n), whole),
                pl.BlockSpec((8, n), whole),
                pl.BlockSpec((8 * SLOTS, n), whole),
            ]
            + [pl.BlockSpec((24, half), whole)] * 4
            + [pl.BlockSpec((48, half), whole)],
            out_specs=[pl.BlockSpec((n, width), whole), pl.BlockSpec((8, n), whole)],
            scratch_shapes=[
                pltpu.VMEM((144, half), F32),
                pltpu.VMEM((8 * SLOTS, 2 * half), BF),
            ],
        ),
        out_shape=[
            jax.ShapeDtypeStruct((n, width), BF),
            jax.ShapeDtypeStruct((8, n), F32),
        ],
        cost_estimate=pl.CostEstimate(
            flops=2 * 64 * n * width, bytes_accessed=4 * n * width, transcendentals=0
        ),
        compiler_params=pltpu.CompilerParams(vmem_limit_bytes=VMEM),
    )(scalars, ids, weights, table, *planes, swapped)


def pieces_product(pieces, rows, flip):
    total = start = 0
    for piece in pieces:
        part = rows[start : start + piece.shape[0]]
        start = start + piece.shape[0]
        pair = (part, piece[...]) if flip else (piece[...], part)
        total = total + lax.dot_general(
            *pair, (((0,), (0,)), ((), ())), preferred_element_type=F32
        )
    return total


def gate_up_kernel(*refs):
    xs, rows, gate, up = refs[:5], refs[5], refs[-2], refs[-1]
    total = pieces_product(xs, rows, False)
    hid = gate.shape[1]
    gate[...] = total[:, :hid].astype(BF)
    up[...] = total[:, hid:].astype(BF)


def down_kernel(*refs):
    ys, hidden, down = refs[:5], *refs[5:]
    down[...] = pieces_product(ys, hidden, True).astype(BF)


def down_grad(pieces, hidden, steps=8):
    width, total, hid = pieces[0].shape[1], *hidden.shape
    block = width // steps
    column = lambda i: (0, i)
    return pl.pallas_call(
        down_kernel,
        grid=(steps,),
        in_specs=[pl.BlockSpec((p.shape[0], block), column) for p in pieces]
        + [pl.BlockSpec((total, hid), lambda i: (0, 0))],
        out_specs=pl.BlockSpec((hid, block), column),
        out_shape=jax.ShapeDtypeStruct((hid, width), BF),
        cost_estimate=pl.CostEstimate(
            flops=2 * total * hid * width,
            bytes_accessed=2 * total * width + 2 * hid * width,
            transcendentals=0,
        ),
        compiler_params=pltpu.CompilerParams(vmem_limit_bytes=VMEM),
    )(*pieces, hidden)


def gate_up_grads(pieces, rows, half, so_far=(), steps=4):
    width, total, cols = pieces[0].shape[1], *rows.shape
    block, hid = width // 2 // steps, cols // 2
    first = half * steps
    return pl.pallas_call(
        gate_up_kernel,
        grid=(steps,),
        in_specs=[
            pl.BlockSpec((p.shape[0], block), lambda i: (0, first + i)) for p in pieces
        ]
        + [pl.BlockSpec((total, cols), lambda i: (0, 0))]
        + [pl.BlockSpec(memory_space=pl.ANY)] * len(so_far),
        out_specs=[pl.BlockSpec((block, hid), lambda i: (first + i, 0))] * 2,
        out_shape=[jax.ShapeDtypeStruct((width, hid), BF)] * 2,
        input_output_aliases={6 + k: k for k in range(len(so_far))},
        cost_estimate=pl.CostEstimate(
            flops=total * cols * width,
            bytes_accessed=total * width + cols * width,
            transcendentals=0,
        ),
        compiler_params=pltpu.CompilerParams(vmem_limit_bytes=VMEM),
    )(*pieces, rows, *so_far)


def join_kernel(place, *refs):
    for i in range(4):
        refs[8 + i][:, :128] = refs[i][...]
        refs[8 + i][:, 128:] = refs[4 + i][...]


def join_weights(place, half, gate, up):
    depth, hid = gate.shape
    size = depth // 8

    def block(i):
        return pl.BlockSpec((size, hid), lambda g, p: (4 * half + (p[0] + i) % 4, 0))

    return pl.pallas_call(
        join_kernel,
        grid_spec=pltpu.PrefetchScalarGridSpec(
            num_scalar_prefetch=1,
            grid=(1,),
            in_specs=[block(i) for i in range(4)] * 2,
            out_specs=[pl.BlockSpec((size, 2 * hid), lambda g, p: (0, 0))] * 4,
        ),
        out_shape=[jax.ShapeDtypeStruct((size, 2 * hid), BF)] * 4,
        cost_estimate=pl.CostEstimate(
            flops=0, bytes_accessed=4 * depth * hid, transcendentals=0
        ),
        compiler_params=pltpu.CompilerParams(vmem_limit_bytes=60 * 2**20),
    )(place, *[gate] * 4, *[up] * 4)


def turn(rows):
    slots = rows.shape[0] // 16
    return rows.reshape(4, 4, slots, -1).swapaxes(0, 1).reshape(rows.shape)


def local(tokens, out_grad, expert_ids, route_weights, w_gate, w_up, w_down):
    width, hid = tokens.shape[1], w_gate.shape[2]
    z, y = lax.axis_index("row") // Y, lax.axis_index("row") % Y
    rel = relative_experts().astype(jnp.int32)
    ids, route_w = expert_ids.T, route_weights.T
    gate, up = w_gate[0], w_up[0]
    own_a, next_a, far_a, last_a = join_weights(z.astype(jnp.int32)[None], 0, gate, up)
    below_a, above_a = shift_z(next_a, 1), shift_z(last_a, -1)
    rel, far_a = lax.optimization_barrier((rel, far_a))
    *planes, table = pack(rel, ids, route_w, tokens, out_grad)
    planes = planes[:1] + [shift_x(p, d + 1) for d, p in enumerate(planes[1:])]
    place_b, table = lax.optimization_barrier((y.astype(jnp.int32)[None], table))
    own_b, next_b, far_b, last_b = join_weights(place_b, 1, gate, up)
    below_a, above_a, next_b, last_b = lax.optimization_barrier(
        (below_a, above_a, next_b, last_b)
    )
    below_b, above_b = shift_y(next_b, 1), shift_y(last_b, -1)
    below_b, above_b, far_a, far_b = lax.optimization_barrier(
        (below_b, above_b, far_a, far_b)
    )
    far_a, far_b = shift_z(far_a, 2), shift_y(far_b, 2)
    gate_up = jnp.concatenate([w_gate[0], w_up[0]], axis=1)
    size = width // 8
    own_x, own_y = assemble(planes, swap_core(other_core(planes)))
    own_x, own_y, far_a, far_b = lax.optimization_barrier((own_x, own_y, far_a, far_b))
    weights_a = jnp.concatenate([own_a, below_a, above_a, far_a], axis=1)
    weights_b = jnp.concatenate([own_b, below_b, above_b, far_b], axis=1)
    ring_x = jnp.concatenate(gather_ring(own_x, shift_z), axis=0)
    ring_y = jnp.concatenate(gather_ring(own_y, shift_y), axis=0)
    parts_x = gather_ring(ring_x, shift_y)
    parts_y = gather_ring(ring_y, shift_z)

    pre = jnp.concatenate(
        [jnp.dot(p, gate_up, preferred_element_type=F32) for p in parts_x], axis=0
    )
    pre_gate, pre_up = pre[:, :hid], pre[:, hid:]
    sig = jax.nn.sigmoid(pre_gate)
    silu = pre_gate * sig
    hidden = (silu * pre_up).astype(BF)
    hidden_grad = turn(
        jnp.concatenate(
            [
                jnp.einsum("rd,hd->rh", p, w_down[0], preferred_element_type=F32)
                for p in parts_y
            ],
            axis=0,
        )
    )
    gate_rows = (hidden_grad * pre_up * sig * (1.0 + pre_gate * (1.0 - sig))).astype(BF)
    up_rows = (hidden_grad * silu).astype(BF)
    rows = jnp.concatenate([gate_rows, up_rows], axis=1)
    route = jnp.sum(hidden.astype(F32) * hidden_grad, axis=1)

    slots = rows.shape[0] // 16
    route_cols = jnp.broadcast_to(route.astype(BF)[:, None], (route.shape[0], 128))
    grad_down = down_grad(parts_y, turn(hidden))
    dx_a = dx_part(rows.reshape(4, 4, slots, -1), weights_a, shift_z)
    dx_b = dx_part(turn(rows).reshape(4, 4, slots, -1), weights_b, shift_y)
    dx_b, rows, grad_down = lax.optimization_barrier((dx_b, rows, grad_down))
    sum_a = sum_over(jnp.concatenate([dx_a, route_cols], axis=1), shift_y)
    sum_b = sum_over(dx_b, shift_z)
    grads = gate_up_grads(parts_x, rows, 0)
    sum_b, grads = lax.optimization_barrier((sum_b, grads))
    own_a = spread(sum_a, shift_z)
    own_b = spread(sum_b, shift_y)
    order = (0, 2, 3, 1)
    to_send = list(regroup([own_a[k] for k in order], [own_b[k] for k in order]))
    to_send, rows = lax.optimization_barrier((to_send, rows))
    back = to_send[:1] + [shift_x(p, -d - 1) for d, p in enumerate(to_send[1:])]
    grad_gate, grad_up = gate_up_grads(parts_x, rows, 1, grads)
    back, grad_gate, grad_up = lax.optimization_barrier((back, grad_gate, grad_up))
    swapped = swap_core(other_core(back, 1))
    scalars = jnp.concatenate([rel, jnp.stack([z, y]).astype(jnp.int32)])
    grad_tokens, grad_route = unpack(scalars, ids, route_w, table, back, swapped)
    return (
        grad_tokens,
        grad_route.T,
        grad_gate[None],
        grad_up[None],
        grad_down[None],
    )


def solution(mesh):
    both = P(("row", "col"), None)
    columns = P("col", None, "row")
    rows = P("col", "row", None)
    return jax.shard_map(
        local,
        mesh=mesh,
        in_specs=(both, both, both, both, columns, columns, rows),
        out_specs=(both, both, columns, columns, rows),
        check_vma=False,
    )
```

```python
import jax
import jax.numpy as jnp
from jax import lax
from jax.experimental import pallas as pl
from jax.experimental.pallas import tpu as pltpu
from jax.sharding import PartitionSpec as P

CAP = 6
Z = 4
Y = 4
X = 4
BF = jnp.bfloat16
F32 = jnp.float32
OFFSETS = (0, -1, 1, 2)
VMEM = 40 * 2**20
SLOTS = 8


def shift_z(value, step):
    pairs = [(z * Y + y, (z + step) % Z * Y + y) for z in range(Z) for y in range(Y)]
    return lax.ppermute(value, "row", pairs)


def shift_y(value, step):
    pairs = [(z * Y + y, z * Y + (y + step) % Y) for z in range(Z) for y in range(Y)]
    return lax.ppermute(value, "row", pairs)


def gather_ring(block, shift):
    half = block.shape[0] // 2
    below = shift(block, 1)
    above = shift(block, -1)
    far_low = shift(below[:half], 1)
    far_high = shift(above[half:], -1)
    return [block, below, above, far_low, far_high]


def gather_direct(block, shift):
    return [block, shift(block, 1), shift(block, -1), shift(block, 2)]


def exchange(blocks, shift):
    return [
        blocks[0],
        shift(blocks[2], 1),
        shift(blocks[1], -1),
        shift(blocks[3], 2),
    ]


def seen_from(rows, offset, axis):
    order = [OFFSETS.index((o - offset + 1) % 4 - 1) for o in OFFSETS]
    return jnp.concatenate(
        [lax.slice_in_dim(rows, k, k + 1, axis=axis) for k in order], axis=axis
    )


def dx_part(rows, weights, shift):
    blocks = gather_direct(rows, shift)
    blocks = [seen_from(b, o, 1) for b, o in zip(blocks, OFFSETS)]
    wide = jnp.concatenate(blocks, axis=3)
    wide = wide.reshape(-1, wide.shape[3])
    return jnp.einsum("rh,dh->rd", wide, weights, preferred_element_type=F32).astype(BF)


def sum_over(part, shift):
    n = part.shape[0] // 4
    pieces = exchange([part[i * n : (i + 1) * n] for i in range(4)], shift)
    return sum(p.astype(F32) for p in pieces).astype(BF)


def spread(part, shift):
    n = part.shape[0] // 4
    return exchange([part[i * n : (i + 1) * n] for i in range(4)], shift)


def relative_experts():
    col = lax.axis_index("col")
    x, core = col // 2, col % 2
    planes = [(x + d) % X for d in range(4)]
    return jnp.stack([2 * plane + c for plane in planes for c in (core, 1 - core)])


def shift_x(value, step):
    pairs = [(x * 2 + c, (x + step) % X * 2 + c) for x in range(X) for c in range(2)]
    return lax.ppermute(value, "col", pairs)


def swap_core(value):
    pairs = [(x * 2 + c, x * 2 + 1 - c) for x in range(X) for c in range(2)]
    return lax.ppermute(value, "col", pairs)


def pack_kernel(rel, ids, weights, tokens, grads, *outs):
    pieces, table_out, table_x, table_y = outs[:4], outs[4], outs[5], outs[6]

    @pl.when(pl.program_id(0) == 0)
    def _():
        n = ids.shape[1]
        expert = lax.broadcasted_iota(jnp.int32, (8, n), 0)
        route = weights[...].astype(F32)
        choose = jnp.zeros((8, n), F32)
        weight = jnp.zeros((8, n), F32)
        for e in range(8):
            hit = ids[...] == rel[e]
            any_hit = jnp.max(jnp.where(hit, 1.0, 0.0), axis=0, keepdims=True)
            total = jnp.sum(jnp.where(hit, route, 0.0), axis=0, keepdims=True)
            choose = jnp.where(expert == e, any_hit, choose)
            weight = jnp.where(expert == e, total, weight)
        earlier = lax.broadcasted_iota(jnp.int32, (n, n), 0) < lax.broadcasted_iota(
            jnp.int32, (n, n), 1
        )
        before = jnp.dot(
            choose.astype(BF), jnp.where(earlier, 1.0, 0.0).astype(BF),
            preferred_element_type=F32,
        )
        spot = jnp.where(choose > 0.0, before, float(CAP))
        spot = jnp.broadcast_to(spot[:, None, :], (8, SLOTS, n))
        row = lax.broadcasted_iota(jnp.int32, (8, SLOTS, n), 1).astype(F32)
        taken = jnp.where((spot == row) & (row < float(CAP)), 1.0, 0.0)
        scaled = taken * jnp.broadcast_to(weight[:, None, :], (8, SLOTS, n))
        taken = taken.reshape(8 * SLOTS, n).astype(BF)
        scaled = scaled.reshape(8 * SLOTS, n).astype(BF)
        table_out[...] = taken
        row = lax.broadcasted_iota(jnp.int32, (96, 8 * SLOTS), 0)
        pad = lax.broadcasted_iota(jnp.int32, (96, 8 * SLOTS), 1)
        same = (row // 12 == pad // SLOTS) & (row % CAP == pad % SLOTS)
        for which, source, out in ((0, taken, table_x), (1, scaled, table_y)):
            pick = jnp.where(same & (row // CAP % 2 == which), 1.0, 0.0).astype(BF)
            out[...] = jnp.dot(pick, source, preferred_element_type=F32).astype(BF)

    rows = jnp.dot(table_x[...], tokens[...], preferred_element_type=F32)
    rows = rows + jnp.dot(table_y[...], grads[...], preferred_element_type=F32)
    for plane in range(4):
        pieces[plane][...] = rows[plane * 24 : plane * 24 + 24].astype(BF)


def pack(rel, ids, weights, tokens, grads, steps=2):
    n, width = tokens.shape
    block = width // steps
    whole = lambda i, rel: (0, 0)
    column = lambda i, rel: (0, i)
    return pl.pallas_call(
        pack_kernel,
        grid_spec=pltpu.PrefetchScalarGridSpec(
            num_scalar_prefetch=1,
            grid=(steps,),
            in_specs=[
                pl.BlockSpec((8, n), whole),
                pl.BlockSpec((8, n), whole),
                pl.BlockSpec((n, block), column),
                pl.BlockSpec((n, block), column),
            ],
            out_specs=[pl.BlockSpec((24, block), column)] * 4
            + [pl.BlockSpec((8 * SLOTS, n), whole)],
            scratch_shapes=[pltpu.VMEM((96, n), BF), pltpu.VMEM((96, n), BF)],
        ),
        out_shape=[jax.ShapeDtypeStruct((24, width), BF)] * 4
        + [jax.ShapeDtypeStruct((8 * SLOTS, n), BF)],
        cost_estimate=pl.CostEstimate(
            flops=4 * 64 * n * width, bytes_accessed=6 * n * width, transcendentals=0
        ),
        compiler_params=pltpu.CompilerParams(vmem_limit_bytes=60 * 2**20),
    )(rel, ids, weights, tokens, grads)


def other_core_kernel(*refs):
    planes, out, held = refs[:4], refs[4], refs[5]
    for plane in range(4):
        held[plane * 24 : plane * 24 + 24] = planes[plane][...].astype(F32)
    row = lax.broadcasted_iota(jnp.int32, (48, 96), 0)
    source = lax.broadcasted_iota(jnp.int32, (48, 96), 1)
    pick = jnp.where(row // 12 * 24 + 12 + row % 12 == source, 1.0, 0.0).astype(BF)
    out[...] = jnp.dot(pick, held[...].astype(BF), preferred_element_type=F32).astype(BF)


def other_core(planes, steps=2):
    width = planes[0].shape[1]
    block = width // steps
    column = lambda i: (0, i)
    return pl.pallas_call(
        other_core_kernel,
        grid=(steps,),
        in_specs=[pl.BlockSpec((24, block), column)] * 4,
        out_specs=pl.BlockSpec((48, block), column),
        scratch_shapes=[pltpu.VMEM((96, block), F32)],
        out_shape=jax.ShapeDtypeStruct((48, width), BF),
        cost_estimate=pl.CostEstimate(
            flops=2 * 48 * 96 * width, bytes_accessed=300 * width, transcendentals=0
        ),
        compiler_params=pltpu.CompilerParams(vmem_limit_bytes=VMEM),
    )(*planes)


def assemble_kernel(*refs):
    planes, swapped, own_x, own_y, held = refs[:4], refs[4], refs[5], refs[6], refs[7]
    for plane in range(4):
        held[plane * 24 : plane * 24 + 24] = planes[plane][...].astype(F32)
    held[96:] = swapped[...].astype(F32)
    rows = held[...].astype(BF)
    row = lax.broadcasted_iota(jnp.int32, (48, 144), 0)
    source = lax.broadcasted_iota(jnp.int32, (48, 144), 1)
    plane, flip, slot = row // 12, row // CAP % 2, row % CAP
    start = jnp.where(flip == 0, plane * 24, 96 + plane * 12) + slot
    for which, out in ((0, own_x), (1, own_y)):
        pick = jnp.where(start + which * CAP == source, 1.0, 0.0).astype(BF)
        out[...] = jnp.dot(pick, rows, preferred_element_type=F32).astype(BF)


def assemble(planes, swapped, steps=2):
    width = swapped.shape[1]
    block = width // steps
    column = lambda i: (0, i)
    return pl.pallas_call(
        assemble_kernel,
        grid=(steps,),
        in_specs=[pl.BlockSpec((24, block), column)] * 4 + [pl.BlockSpec((48, block), column)],
        out_specs=[pl.BlockSpec((8 * CAP, block), column)] * 2,
        scratch_shapes=[pltpu.VMEM((144, block), F32)],
        out_shape=[jax.ShapeDtypeStruct((8 * CAP, width), BF)] * 2,
        cost_estimate=pl.CostEstimate(
            flops=4 * 144 * 48 * width, bytes_accessed=500 * width, transcendentals=0
        ),
        compiler_params=pltpu.CompilerParams(vmem_limit_bytes=VMEM),
    )(*planes, swapped)


def regroup_kernel(*refs):
    own, outs, held = refs[:8], refs[8:12], refs[12]
    size = own[4].shape[1]
    for j in range(8):
        held[:, j * size : (j + 1) * size] = own[j][:, :size]
    route = sum(own[j][:, size:].astype(F32) for j in range(4)).astype(BF)
    held[:, 8 * size : 8 * size + 128] = route
    held[:, 8 * size + 128 :] = route
    half = outs[0].shape[1]
    row = lax.broadcasted_iota(jnp.int32, (96, 8 * CAP), 0)
    source = lax.broadcasted_iota(jnp.int32, (96, 8 * CAP), 1)
    total = 0.0
    for which in range(2):
        pick = (row // 12 * CAP + row % CAP == source) & (row // CAP % 2 == which)
        total = total + jnp.dot(
            jnp.where(pick, 1.0, 0.0).astype(BF),
            held[:, which * half : (which + 1) * half],
            preferred_element_type=F32,
        )
    for plane in range(4):
        outs[plane][...] = total[plane * 24 : plane * 24 + 24].astype(BF)


def regroup(own_a, own_b):
    width = 8 * own_b[0].shape[1] + 256
    return pl.pallas_call(
        regroup_kernel,
        out_shape=[jax.ShapeDtypeStruct((24, width // 2), BF)] * 4,
        scratch_shapes=[pltpu.VMEM((8 * CAP, width), BF)],
        cost_estimate=pl.CostEstimate(
            flops=4 * 96 * 48 * width, bytes_accessed=4 * 48 * width, transcendentals=0
        ),
        compiler_params=pltpu.CompilerParams(vmem_limit_bytes=VMEM),
    )(*own_a, *own_b)


def unpack_kernel(scalars, ids, weights, table, *refs):
    planes, swapped, grads, route_out, held, padded = refs[:4], refs[4], *refs[5:]
    n, width = ids.shape[1], grads.shape[1]
    size, half = width // 8, swapped.shape[1]
    for plane in range(4):
        held[plane * 24 : plane * 24 + 24] = planes[plane][...].astype(F32)
    held[96:] = swapped[...].astype(F32)
    rows = held[...].astype(BF)
    row = lax.broadcasted_iota(jnp.int32, (8 * SLOTS, 144), 0)
    source = lax.broadcasted_iota(jnp.int32, (8 * SLOTS, 144), 1)
    plane, flip, slot = row // 16, row // SLOTS % 2, row % SLOTS
    start = jnp.where(flip == 0, plane * 24, 96 + plane * 12) + slot
    for which in range(2):
        pick = (start + which * CAP == source) & (slot < CAP)
        padded[:, which * half : (which + 1) * half] = jnp.dot(
            jnp.where(pick, 1.0, 0.0).astype(BF), rows, preferred_element_type=F32
        ).astype(BF)

    per_slot = table[...].astype(F32) * padded[:, width : width + 1].astype(F32)
    per_expert = jnp.sum(per_slot.reshape(8, SLOTS, n), axis=1)
    total = jnp.zeros((8, n), F32)
    for e in range(8):
        total = total + jnp.where(ids[...] == scalars[e], per_expert[e : e + 1], 0.0)
    route_out[...] = total / weights[...].astype(F32)
    for j in range(8):
        at = (j + scalars[8]) % 4 if j < 4 else 4 + (j + scalars[9]) % 4
        grads[:, pl.ds(pl.multiple_of(at * size, 128), size)] = lax.dot_general(
            table[...], padded[:, j * size : (j + 1) * size], (((0,), (0,)), ((), ())),
            preferred_element_type=F32,
        ).astype(BF)


def unpack(scalars, ids, weights, table, planes, swapped):
    n, half = ids.shape[1], swapped.shape[1]
    width = 2 * half - 256
    whole = lambda i, s: (0, 0)
    return pl.pallas_call(
        unpack_kernel,
        grid_spec=pltpu.PrefetchScalarGridSpec(
            num_scalar_prefetch=1,
            grid=(1,),
            in_specs=[
                pl.BlockSpec((8, n), whole),
                pl.BlockSpec((8, n), whole),
                pl.BlockSpec((8 * SLOTS, n), whole),
            ]
            + [pl.BlockSpec((24, half), whole)] * 4
            + [pl.BlockSpec((48, half), whole)],
            out_specs=[pl.BlockSpec((n, width), whole), pl.BlockSpec((8, n), whole)],
            scratch_shapes=[
                pltpu.VMEM((144, half), F32),
                pltpu.VMEM((8 * SLOTS, 2 * half), BF),
            ],
        ),
        out_shape=[
            jax.ShapeDtypeStruct((n, width), BF),
            jax.ShapeDtypeStruct((8, n), F32),
        ],
        cost_estimate=pl.CostEstimate(
            flops=2 * 64 * n * width, bytes_accessed=4 * n * width, transcendentals=0
        ),
        compiler_params=pltpu.CompilerParams(vmem_limit_bytes=VMEM),
    )(scalars, ids, weights, table, *planes, swapped)


def pieces_product(pieces, rows, flip):
    total = start = 0
    for piece in pieces:
        part = rows[start : start + piece.shape[0]]
        start = start + piece.shape[0]
        pair = (part, piece[...]) if flip else (piece[...], part)
        total = total + lax.dot_general(
            *pair, (((0,), (0,)), ((), ())), preferred_element_type=F32
        )
    return total


def gate_up_kernel(*refs):
    xs, rows, gate, up = refs[:5], refs[5], refs[-2], refs[-1]
    total = pieces_product(xs, rows, False)
    hid = gate.shape[1]
    gate[...] = total[:, :hid].astype(BF)
    up[...] = total[:, hid:].astype(BF)


def down_kernel(*refs):
    ys, hidden, down = refs[:5], *refs[5:]
    down[...] = pieces_product(ys, hidden, True).astype(BF)


def down_grad(pieces, hidden, steps=8):
    width, total, hid = pieces[0].shape[1], *hidden.shape
    block = width // steps
    column = lambda i: (0, i)
    return pl.pallas_call(
        down_kernel,
        grid=(steps,),
        in_specs=[pl.BlockSpec((p.shape[0], block), column) for p in pieces]
        + [pl.BlockSpec((total, hid), lambda i: (0, 0))],
        out_specs=pl.BlockSpec((hid, block), column),
        out_shape=jax.ShapeDtypeStruct((hid, width), BF),
        cost_estimate=pl.CostEstimate(
            flops=2 * total * hid * width,
            bytes_accessed=2 * total * width + 2 * hid * width,
            transcendentals=0,
        ),
        compiler_params=pltpu.CompilerParams(vmem_limit_bytes=VMEM),
    )(*pieces, hidden)


def gate_up_grads(pieces, rows, half, so_far=(), steps=4):
    width, total, cols = pieces[0].shape[1], *rows.shape
    block, hid = width // 2 // steps, cols // 2
    first = half * steps
    return pl.pallas_call(
        gate_up_kernel,
        grid=(steps,),
        in_specs=[
            pl.BlockSpec((p.shape[0], block), lambda i: (0, first + i)) for p in pieces
        ]
        + [pl.BlockSpec((total, cols), lambda i: (0, 0))]
        + [pl.BlockSpec(memory_space=pl.ANY)] * len(so_far),
        out_specs=[pl.BlockSpec((block, hid), lambda i: (first + i, 0))] * 2,
        out_shape=[jax.ShapeDtypeStruct((width, hid), BF)] * 2,
        input_output_aliases={6 + k: k for k in range(len(so_far))},
        cost_estimate=pl.CostEstimate(
            flops=total * cols * width,
            bytes_accessed=total * width + cols * width,
            transcendentals=0,
        ),
        compiler_params=pltpu.CompilerParams(vmem_limit_bytes=VMEM),
    )(*pieces, rows, *so_far)


def join_kernel(place, *refs):
    for i in range(4):
        refs[8 + i][:, :128] = refs[i][...]
        refs[8 + i][:, 128:] = refs[4 + i][...]


def join_weights(place, half, gate, up):
    depth, hid = gate.shape
    size = depth // 8

    def block(i):
        return pl.BlockSpec((size, hid), lambda g, p: (4 * half + (p[0] + i) % 4, 0))

    return pl.pallas_call(
        join_kernel,
        grid_spec=pltpu.PrefetchScalarGridSpec(
            num_scalar_prefetch=1,
            grid=(1,),
            in_specs=[block(i) for i in range(4)] * 2,
            out_specs=[pl.BlockSpec((size, 2 * hid), lambda g, p: (0, 0))] * 4,
        ),
        out_shape=[jax.ShapeDtypeStruct((size, 2 * hid), BF)] * 4,
        cost_estimate=pl.CostEstimate(
            flops=0, bytes_accessed=4 * depth * hid, transcendentals=0
        ),
        compiler_params=pltpu.CompilerParams(vmem_limit_bytes=60 * 2**20),
    )(place, *[gate] * 4, *[up] * 4)


def turn(rows):
    slots = rows.shape[0] // 16
    return rows.reshape(4, 4, slots, -1).swapaxes(0, 1).reshape(rows.shape)


def local(tokens, out_grad, expert_ids, route_weights, w_gate, w_up, w_down):
    width, hid = tokens.shape[1], w_gate.shape[2]
    z, y = lax.axis_index("row") // Y, lax.axis_index("row") % Y
    rel = relative_experts().astype(jnp.int32)
    ids, route_w = expert_ids.T, route_weights.T
    gate, up = w_gate[0], w_up[0]
    own_a, next_a, far_a, last_a = join_weights(z.astype(jnp.int32)[None], 0, gate, up)
    below_a, above_a = shift_z(next_a, 1), shift_z(last_a, -1)
    rel, far_a = lax.optimization_barrier((rel, far_a))
    *planes, table = pack(rel, ids, route_w, tokens, out_grad)
    planes = planes[:1] + [shift_x(p, d + 1) for d, p in enumerate(planes[1:])]
    place_b, table = lax.optimization_barrier((y.astype(jnp.int32)[None], table))
    own_b, next_b, far_b, last_b = join_weights(place_b, 1, gate, up)
    below_a, above_a, next_b, last_b = lax.optimization_barrier(
        (below_a, above_a, next_b, last_b)
    )
    below_b, above_b = shift_y(next_b, 1), shift_y(last_b, -1)
    below_b, above_b, far_a, far_b = lax.optimization_barrier(
        (below_b, above_b, far_a, far_b)
    )
    far_a, far_b = shift_z(far_a, 2), shift_y(far_b, 2)
    gate_up = jnp.concatenate([w_gate[0], w_up[0]], axis=1)
    size = width // 8
    own_x, own_y = assemble(planes, swap_core(other_core(planes)))
    own_x, own_y, far_a, far_b = lax.optimization_barrier((own_x, own_y, far_a, far_b))
    weights_a = jnp.concatenate([own_a, below_a, above_a, far_a], axis=1)
    weights_b = jnp.concatenate([own_b, below_b, above_b, far_b], axis=1)
    ring_x = jnp.concatenate(gather_ring(own_x, shift_z), axis=0)
    ring_y = jnp.concatenate(gather_ring(own_y, shift_y), axis=0)
    ring_y, _ = lax.optimization_barrier((ring_y, ring_x))
    parts_x = gather_ring(ring_x, shift_y)
    parts_y = gather_ring(ring_y, shift_z)

    pre = jnp.concatenate(
        [jnp.dot(p, gate_up, preferred_element_type=F32) for p in parts_x], axis=0
    )
    pre_gate, pre_up = pre[:, :hid], pre[:, hid:]
    sig = jax.nn.sigmoid(pre_gate)
    silu = pre_gate * sig
    hidden = (silu * pre_up).astype(BF)
    hidden_grad = turn(
        jnp.concatenate(
            [
                jnp.einsum("rd,hd->rh", p, w_down[0], preferred_element_type=F32)
                for p in parts_y
            ],
            axis=0,
        )
    )
    gate_rows = (hidden_grad * pre_up * sig * (1.0 + pre_gate * (1.0 - sig))).astype(BF)
    up_rows = (hidden_grad * silu).astype(BF)
    rows = jnp.concatenate([gate_rows, up_rows], axis=1)
    route = jnp.sum(hidden.astype(F32) * hidden_grad, axis=1)

    slots = rows.shape[0] // 16
    route_cols = jnp.broadcast_to(route.astype(BF)[:, None], (route.shape[0], 128))
    grad_down = down_grad(parts_y, turn(hidden))
    dx_a = dx_part(rows.reshape(4, 4, slots, -1), weights_a, shift_z)
    dx_b = dx_part(turn(rows).reshape(4, 4, slots, -1), weights_b, shift_y)
    dx_b, rows, grad_down = lax.optimization_barrier((dx_b, rows, grad_down))
    sum_a = sum_over(jnp.concatenate([dx_a, route_cols], axis=1), shift_y)
    sum_b = sum_over(dx_b, shift_z)
    grads = gate_up_grads(parts_x, rows, 0)
    sum_b, grads = lax.optimization_barrier((sum_b, grads))
    own_a = spread(sum_a, shift_z)
    own_b = spread(sum_b, shift_y)
    order = (0, 2, 3, 1)
    to_send = list(regroup([own_a[k] for k in order], [own_b[k] for k in order]))
    to_send, rows = lax.optimization_barrier((to_send, rows))
    back = to_send[:1] + [shift_x(p, -d - 1) for d, p in enumerate(to_send[1:])]
    grad_gate, grad_up = gate_up_grads(parts_x, rows, 1, grads)
    back, grad_gate, grad_up = lax.optimization_barrier((back, grad_gate, grad_up))
    swapped = swap_core(other_core(back, 1))
    scalars = jnp.concatenate([rel, jnp.stack([z, y]).astype(jnp.int32)])
    grad_tokens, grad_route = unpack(scalars, ids, route_w, table, back, swapped)
    return (
        grad_tokens,
        grad_route.T,
        grad_gate[None],
        grad_up[None],
        grad_down[None],
    )


def solution(mesh):
    both = P(("row", "col"), None)
    columns = P("col", None, "row")
    rows = P("col", "row", None)
    return jax.shard_map(
        local,
        mesh=mesh,
        in_specs=(both, both, both, both, columns, columns, rows),
        out_specs=(both, both, columns, columns, rows),
        check_vma=False,
    )
```

```python
import jax
import jax.numpy as jnp
from jax import lax
from jax.experimental import pallas as pl
from jax.experimental.pallas import tpu as pltpu
from jax.sharding import PartitionSpec as P

CAP = 6
Z = 4
Y = 4
X = 4
BF = jnp.bfloat16
F32 = jnp.float32
OFFSETS = (0, -1, 1, 2)
VMEM = 40 * 2**20
SLOTS = 8


def shift_z(value, step):
    pairs = [(z * Y + y, (z + step) % Z * Y + y) for z in range(Z) for y in range(Y)]
    return lax.ppermute(value, "row", pairs)


def shift_y(value, step):
    pairs = [(z * Y + y, z * Y + (y + step) % Y) for z in range(Z) for y in range(Y)]
    return lax.ppermute(value, "row", pairs)


def gather_ring(block, shift):
    half = block.shape[0] // 2
    below = shift(block, 1)
    above = shift(block, -1)
    far_low = shift(below[:half], 1)
    far_high = shift(above[half:], -1)
    return [block, below, above, far_low, far_high]


def gather_direct(block, shift):
    return [block, shift(block, 1), shift(block, -1), shift(block, 2)]


def exchange(blocks, shift):
    return [
        blocks[0],
        shift(blocks[2], 1),
        shift(blocks[1], -1),
        shift(blocks[3], 2),
    ]


def seen_from(rows, offset, axis):
    order = [OFFSETS.index((o - offset + 1) % 4 - 1) for o in OFFSETS]
    return jnp.concatenate(
        [lax.slice_in_dim(rows, k, k + 1, axis=axis) for k in order], axis=axis
    )


def dx_part(rows, weights, shift):
    blocks = gather_direct(rows, shift)
    blocks = [seen_from(b, o, 1) for b, o in zip(blocks, OFFSETS)]
    wide = jnp.concatenate(blocks, axis=3)
    wide = wide.reshape(-1, wide.shape[3])
    return jnp.einsum("rh,dh->rd", wide, weights, preferred_element_type=F32).astype(BF)


def sum_over(part, shift):
    n = part.shape[0] // 4
    pieces = exchange([part[i * n : (i + 1) * n] for i in range(4)], shift)
    return sum(p.astype(F32) for p in pieces).astype(BF)


def spread(part, shift):
    n = part.shape[0] // 4
    return exchange([part[i * n : (i + 1) * n] for i in range(4)], shift)


def relative_experts():
    col = lax.axis_index("col")
    x, core = col // 2, col % 2
    planes = [(x + d) % X for d in range(4)]
    return jnp.stack([2 * plane + c for plane in planes for c in (core, 1 - core)])


def shift_x(value, step):
    pairs = [(x * 2 + c, (x + step) % X * 2 + c) for x in range(X) for c in range(2)]
    return lax.ppermute(value, "col", pairs)


def swap_core(value):
    pairs = [(x * 2 + c, x * 2 + 1 - c) for x in range(X) for c in range(2)]
    return lax.ppermute(value, "col", pairs)


def pack_kernel(rel, ids, weights, tokens, grads, *outs):
    pieces, table_out, table_x, table_y = outs[:4], outs[4], outs[5], outs[6]

    @pl.when(pl.program_id(0) == 0)
    def _():
        n = ids.shape[1]
        expert = lax.broadcasted_iota(jnp.int32, (8, n), 0)
        route = weights[...].astype(F32)
        choose = jnp.zeros((8, n), F32)
        weight = jnp.zeros((8, n), F32)
        for e in range(8):
            hit = ids[...] == rel[e]
            any_hit = jnp.max(jnp.where(hit, 1.0, 0.0), axis=0, keepdims=True)
            total = jnp.sum(jnp.where(hit, route, 0.0), axis=0, keepdims=True)
            choose = jnp.where(expert == e, any_hit, choose)
            weight = jnp.where(expert == e, total, weight)
        earlier = lax.broadcasted_iota(jnp.int32, (n, n), 0) < lax.broadcasted_iota(
            jnp.int32, (n, n), 1
        )
        before = jnp.dot(
            choose.astype(BF), jnp.where(earlier, 1.0, 0.0).astype(BF),
            preferred_element_type=F32,
        )
        spot = jnp.where(choose > 0.0, before, float(CAP))
        spot = jnp.broadcast_to(spot[:, None, :], (8, SLOTS, n))
        row = lax.broadcasted_iota(jnp.int32, (8, SLOTS, n), 1).astype(F32)
        taken = jnp.where((spot == row) & (row < float(CAP)), 1.0, 0.0)
        scaled = taken * jnp.broadcast_to(weight[:, None, :], (8, SLOTS, n))
        taken = taken.reshape(8 * SLOTS, n).astype(BF)
        scaled = scaled.reshape(8 * SLOTS, n).astype(BF)
        table_out[...] = taken
        row = lax.broadcasted_iota(jnp.int32, (96, 8 * SLOTS), 0)
        pad = lax.broadcasted_iota(jnp.int32, (96, 8 * SLOTS), 1)
        same = (row // 12 == pad // SLOTS) & (row % CAP == pad % SLOTS)
        for which, source, out in ((0, taken, table_x), (1, scaled, table_y)):
            pick = jnp.where(same & (row // CAP % 2 == which), 1.0, 0.0).astype(BF)
            out[...] = jnp.dot(pick, source, preferred_element_type=F32).astype(BF)

    rows = jnp.dot(table_x[...], tokens[...], preferred_element_type=F32)
    rows = rows + jnp.dot(table_y[...], grads[...], preferred_element_type=F32)
    for plane in range(4):
        pieces[plane][...] = rows[plane * 24 : plane * 24 + 24].astype(BF)


def pack(rel, ids, weights, tokens, grads, steps=2):
    n, width = tokens.shape
    block = width // steps
    whole = lambda i, rel: (0, 0)
    column = lambda i, rel: (0, i)
    return pl.pallas_call(
        pack_kernel,
        grid_spec=pltpu.PrefetchScalarGridSpec(
            num_scalar_prefetch=1,
            grid=(steps,),
            in_specs=[
                pl.BlockSpec((8, n), whole),
                pl.BlockSpec((8, n), whole),
                pl.BlockSpec((n, block), column),
                pl.BlockSpec((n, block), column),
            ],
            out_specs=[pl.BlockSpec((24, block), column)] * 4
            + [pl.BlockSpec((8 * SLOTS, n), whole)],
            scratch_shapes=[pltpu.VMEM((96, n), BF), pltpu.VMEM((96, n), BF)],
        ),
        out_shape=[jax.ShapeDtypeStruct((24, width), BF)] * 4
        + [jax.ShapeDtypeStruct((8 * SLOTS, n), BF)],
        cost_estimate=pl.CostEstimate(
            flops=4 * 64 * n * width, bytes_accessed=6 * n * width, transcendentals=0
        ),
        compiler_params=pltpu.CompilerParams(vmem_limit_bytes=60 * 2**20),
    )(rel, ids, weights, tokens, grads)


def other_core_kernel(*refs):
    planes, out, held = refs[:4], refs[4], refs[5]
    for plane in range(4):
        held[plane * 24 : plane * 24 + 24] = planes[plane][...].astype(F32)
    row = lax.broadcasted_iota(jnp.int32, (48, 96), 0)
    source = lax.broadcasted_iota(jnp.int32, (48, 96), 1)
    pick = jnp.where(row // 12 * 24 + 12 + row % 12 == source, 1.0, 0.0).astype(BF)
    out[...] = jnp.dot(pick, held[...].astype(BF), preferred_element_type=F32).astype(BF)


def other_core(planes, steps=2):
    width = planes[0].shape[1]
    block = width // steps
    column = lambda i: (0, i)
    return pl.pallas_call(
        other_core_kernel,
        grid=(steps,),
        in_specs=[pl.BlockSpec((24, block), column)] * 4,
        out_specs=pl.BlockSpec((48, block), column),
        scratch_shapes=[pltpu.VMEM((96, block), F32)],
        out_shape=jax.ShapeDtypeStruct((48, width), BF),
        cost_estimate=pl.CostEstimate(
            flops=2 * 48 * 96 * width, bytes_accessed=300 * width, transcendentals=0
        ),
        compiler_params=pltpu.CompilerParams(vmem_limit_bytes=VMEM),
    )(*planes)


def assemble_kernel(*refs):
    planes, swapped, own_x, own_y, held = refs[:4], refs[4], refs[5], refs[6], refs[7]
    for plane in range(4):
        held[plane * 24 : plane * 24 + 24] = planes[plane][...].astype(F32)
    held[96:] = swapped[...].astype(F32)
    rows = held[...].astype(BF)
    row = lax.broadcasted_iota(jnp.int32, (48, 144), 0)
    source = lax.broadcasted_iota(jnp.int32, (48, 144), 1)
    plane, flip, slot = row // 12, row // CAP % 2, row % CAP
    start = jnp.where(flip == 0, plane * 24, 96 + plane * 12) + slot
    for which, out in ((0, own_x), (1, own_y)):
        pick = jnp.where(start + which * CAP == source, 1.0, 0.0).astype(BF)
        out[...] = jnp.dot(pick, rows, preferred_element_type=F32).astype(BF)


def assemble(planes, swapped, steps=2):
    width = swapped.shape[1]
    block = width // steps
    column = lambda i: (0, i)
    return pl.pallas_call(
        assemble_kernel,
        grid=(steps,),
        in_specs=[pl.BlockSpec((24, block), column)] * 4 + [pl.BlockSpec((48, block), column)],
        out_specs=[pl.BlockSpec((8 * CAP, block), column)] * 2,
        scratch_shapes=[pltpu.VMEM((144, block), F32)],
        out_shape=[jax.ShapeDtypeStruct((8 * CAP, width), BF)] * 2,
        cost_estimate=pl.CostEstimate(
            flops=4 * 144 * 48 * width, bytes_accessed=500 * width, transcendentals=0
        ),
        compiler_params=pltpu.CompilerParams(vmem_limit_bytes=VMEM),
    )(*planes, swapped)


def regroup_kernel(*refs):
    own, outs, held = refs[:8], refs[8:12], refs[12]
    size = own[4].shape[1]
    for j in range(8):
        held[:, j * size : (j + 1) * size] = own[j][:, :size]
    route = sum(own[j][:, size:].astype(F32) for j in range(4)).astype(BF)
    held[:, 8 * size : 8 * size + 128] = route
    held[:, 8 * size + 128 :] = route
    half = outs[0].shape[1]
    row = lax.broadcasted_iota(jnp.int32, (96, 8 * CAP), 0)
    source = lax.broadcasted_iota(jnp.int32, (96, 8 * CAP), 1)
    total = 0.0
    for which in range(2):
        pick = (row // 12 * CAP + row % CAP == source) & (row // CAP % 2 == which)
        total = total + jnp.dot(
            jnp.where(pick, 1.0, 0.0).astype(BF),
            held[:, which * half : (which + 1) * half],
            preferred_element_type=F32,
        )
    for plane in range(4):
        outs[plane][...] = total[plane * 24 : plane * 24 + 24].astype(BF)


def regroup(own_a, own_b):
    width = 8 * own_b[0].shape[1] + 256
    return pl.pallas_call(
        regroup_kernel,
        out_shape=[jax.ShapeDtypeStruct((24, width // 2), BF)] * 4,
        scratch_shapes=[pltpu.VMEM((8 * CAP, width), BF)],
        cost_estimate=pl.CostEstimate(
            flops=4 * 96 * 48 * width, bytes_accessed=4 * 48 * width, transcendentals=0
        ),
        compiler_params=pltpu.CompilerParams(vmem_limit_bytes=VMEM),
    )(*own_a, *own_b)


def unpack_kernel(scalars, ids, weights, table, *refs):
    planes, swapped, grads, route_out, held, padded = refs[:4], refs[4], *refs[5:]
    n, width = ids.shape[1], grads.shape[1]
    size, half = width // 8, swapped.shape[1]
    for plane in range(4):
        held[plane * 24 : plane * 24 + 24] = planes[plane][...].astype(F32)
    held[96:] = swapped[...].astype(F32)
    rows = held[...].astype(BF)
    row = lax.broadcasted_iota(jnp.int32, (8 * SLOTS, 144), 0)
    source = lax.broadcasted_iota(jnp.int32, (8 * SLOTS, 144), 1)
    plane, flip, slot = row // 16, row // SLOTS % 2, row % SLOTS
    start = jnp.where(flip == 0, plane * 24, 96 + plane * 12) + slot
    for which in range(2):
        pick = (start + which * CAP == source) & (slot < CAP)
        padded[:, which * half : (which + 1) * half] = jnp.dot(
            jnp.where(pick, 1.0, 0.0).astype(BF), rows, preferred_element_type=F32
        ).astype(BF)

    per_slot = table[...].astype(F32) * padded[:, width : width + 1].astype(F32)
    per_expert = jnp.sum(per_slot.reshape(8, SLOTS, n), axis=1)
    total = jnp.zeros((8, n), F32)
    for e in range(8):
        total = total + jnp.where(ids[...] == scalars[e], per_expert[e : e + 1], 0.0)
    route_out[...] = total / weights[...].astype(F32)
    for j in range(8):
        at = (j + scalars[8]) % 4 if j < 4 else 4 + (j + scalars[9]) % 4
        grads[:, pl.ds(pl.multiple_of(at * size, 128), size)] = lax.dot_general(
            table[...], padded[:, j * size : (j + 1) * size], (((0,), (0,)), ((), ())),
            preferred_element_type=F32,
        ).astype(BF)


def unpack(scalars, ids, weights, table, planes, swapped):
    n, half = ids.shape[1], swapped.shape[1]
    width = 2 * half - 256
    whole = lambda i, s: (0, 0)
    return pl.pallas_call(
        unpack_kernel,
        grid_spec=pltpu.PrefetchScalarGridSpec(
            num_scalar_prefetch=1,
            grid=(1,),
            in_specs=[
                pl.BlockSpec((8, n), whole),
                pl.BlockSpec((8, n), whole),
                pl.BlockSpec((8 * SLOTS, n), whole),
            ]
            + [pl.BlockSpec((24, half), whole)] * 4
            + [pl.BlockSpec((48, half), whole)],
            out_specs=[pl.BlockSpec((n, width), whole), pl.BlockSpec((8, n), whole)],
            scratch_shapes=[
                pltpu.VMEM((144, half), F32),
                pltpu.VMEM((8 * SLOTS, 2 * half), BF),
            ],
        ),
        out_shape=[
            jax.ShapeDtypeStruct((n, width), BF),
            jax.ShapeDtypeStruct((8, n), F32),
        ],
        cost_estimate=pl.CostEstimate(
            flops=2 * 64 * n * width, bytes_accessed=4 * n * width, transcendentals=0
        ),
        compiler_params=pltpu.CompilerParams(vmem_limit_bytes=VMEM),
    )(scalars, ids, weights, table, *planes, swapped)


def pieces_product(pieces, rows, flip):
    total = start = 0
    for piece in pieces:
        part = rows[start : start + piece.shape[0]]
        start = start + piece.shape[0]
        pair = (part, piece[...]) if flip else (piece[...], part)
        total = total + lax.dot_general(
            *pair, (((0,), (0,)), ((), ())), preferred_element_type=F32
        )
    return total


def gate_up_kernel(*refs):
    xs, rows, gate, up = refs[:5], refs[5], refs[-2], refs[-1]
    total = pieces_product(xs, rows, False)
    hid = gate.shape[1]
    gate[...] = total[:, :hid].astype(BF)
    up[...] = total[:, hid:].astype(BF)


def down_kernel(*refs):
    ys, hidden, down = refs[:5], *refs[5:]
    down[...] = pieces_product(ys, hidden, True).astype(BF)


def down_grad(pieces, hidden, steps=8):
    width, total, hid = pieces[0].shape[1], *hidden.shape
    block = width // steps
    column = lambda i: (0, i)
    return pl.pallas_call(
        down_kernel,
        grid=(steps,),
        in_specs=[pl.BlockSpec((p.shape[0], block), column) for p in pieces]
        + [pl.BlockSpec((total, hid), lambda i: (0, 0))],
        out_specs=pl.BlockSpec((hid, block), column),
        out_shape=jax.ShapeDtypeStruct((hid, width), BF),
        cost_estimate=pl.CostEstimate(
            flops=2 * total * hid * width,
            bytes_accessed=2 * total * width + 2 * hid * width,
            transcendentals=0,
        ),
        compiler_params=pltpu.CompilerParams(vmem_limit_bytes=VMEM),
    )(*pieces, hidden)


def gate_up_grads(pieces, rows, half, so_far=(), steps=4):
    width, total, cols = pieces[0].shape[1], *rows.shape
    block, hid = width // 2 // steps, cols // 2
    first = half * steps
    return pl.pallas_call(
        gate_up_kernel,
        grid=(steps,),
        in_specs=[
            pl.BlockSpec((p.shape[0], block), lambda i: (0, first + i)) for p in pieces
        ]
        + [pl.BlockSpec((total, cols), lambda i: (0, 0))]
        + [pl.BlockSpec(memory_space=pl.ANY)] * len(so_far),
        out_specs=[pl.BlockSpec((block, hid), lambda i: (first + i, 0))] * 2,
        out_shape=[jax.ShapeDtypeStruct((width, hid), BF)] * 2,
        input_output_aliases={6 + k: k for k in range(len(so_far))},
        cost_estimate=pl.CostEstimate(
            flops=total * cols * width,
            bytes_accessed=total * width + cols * width,
            transcendentals=0,
        ),
        compiler_params=pltpu.CompilerParams(vmem_limit_bytes=VMEM),
    )(*pieces, rows, *so_far)


def join_kernel(place, *refs):
    for i in range(4):
        refs[8 + i][:, :128] = refs[i][...]
        refs[8 + i][:, 128:] = refs[4 + i][...]


def join_weights(place, half, gate, up):
    depth, hid = gate.shape
    size = depth // 8

    def block(i):
        return pl.BlockSpec((size, hid), lambda g, p: (4 * half + (p[0] + i) % 4, 0))

    return pl.pallas_call(
        join_kernel,
        grid_spec=pltpu.PrefetchScalarGridSpec(
            num_scalar_prefetch=1,
            grid=(1,),
            in_specs=[block(i) for i in range(4)] * 2,
            out_specs=[pl.BlockSpec((size, 2 * hid), lambda g, p: (0, 0))] * 4,
        ),
        out_shape=[jax.ShapeDtypeStruct((size, 2 * hid), BF)] * 4,
        cost_estimate=pl.CostEstimate(
            flops=0, bytes_accessed=4 * depth * hid, transcendentals=0
        ),
        compiler_params=pltpu.CompilerParams(vmem_limit_bytes=60 * 2**20),
    )(place, *[gate] * 4, *[up] * 4)


def turn(rows):
    slots = rows.shape[0] // 16
    return rows.reshape(4, 4, slots, -1).swapaxes(0, 1).reshape(rows.shape)


def local(tokens, out_grad, expert_ids, route_weights, w_gate, w_up, w_down):
    width, hid = tokens.shape[1], w_gate.shape[2]
    z, y = lax.axis_index("row") // Y, lax.axis_index("row") % Y
    rel = relative_experts().astype(jnp.int32)
    ids, route_w = expert_ids.T, route_weights.T
    gate, up = w_gate[0], w_up[0]
    own_a, next_a, far_a, last_a = join_weights(z.astype(jnp.int32)[None], 0, gate, up)
    below_a, above_a = shift_z(next_a, 1), shift_z(last_a, -1)
    rel, far_a = lax.optimization_barrier((rel, far_a))
    *planes, table = pack(rel, ids, route_w, tokens, out_grad)
    planes = planes[:1] + [shift_x(p, d + 1) for d, p in enumerate(planes[1:])]
    place_b, table = lax.optimization_barrier((y.astype(jnp.int32)[None], table))
    own_b, next_b, far_b, last_b = join_weights(place_b, 1, gate, up)
    below_a, above_a, next_b, last_b = lax.optimization_barrier(
        (below_a, above_a, next_b, last_b)
    )
    below_b, above_b = shift_y(next_b, 1), shift_y(last_b, -1)
    planes, below_b, above_b, far_a, far_b = lax.optimization_barrier(
        (planes, below_b, above_b, far_a, far_b)
    )
    far_a, far_b = shift_z(far_a, 2), shift_y(far_b, 2)
    gate_up = jnp.concatenate([w_gate[0], w_up[0]], axis=1)
    size = width // 8
    own_x, own_y = assemble(planes, swap_core(other_core(planes)))
    own_x, own_y, far_a, far_b = lax.optimization_barrier((own_x, own_y, far_a, far_b))
    weights_a = jnp.concatenate([own_a, below_a, above_a, far_a], axis=1)
    weights_b = jnp.concatenate([own_b, below_b, above_b, far_b], axis=1)
    ring_x = jnp.concatenate(gather_ring(own_x, shift_z), axis=0)
    ring_y = jnp.concatenate(gather_ring(own_y, shift_y), axis=0)
    ring_y, _ = lax.optimization_barrier((ring_y, ring_x))
    parts_x = gather_ring(ring_x, shift_y)
    parts_y = gather_ring(ring_y, shift_z)

    pre = jnp.concatenate(
        [jnp.dot(p, gate_up, preferred_element_type=F32) for p in parts_x], axis=0
    )
    pre_gate, pre_up = pre[:, :hid], pre[:, hid:]
    sig = jax.nn.sigmoid(pre_gate)
    silu = pre_gate * sig
    hidden = (silu * pre_up).astype(BF)
    hidden_grad = turn(
        jnp.concatenate(
            [
                jnp.einsum("rd,hd->rh", p, w_down[0], preferred_element_type=F32)
                for p in parts_y
            ],
            axis=0,
        )
    )
    gate_rows = (hidden_grad * pre_up * sig * (1.0 + pre_gate * (1.0 - sig))).astype(BF)
    up_rows = (hidden_grad * silu).astype(BF)
    rows = jnp.concatenate([gate_rows, up_rows], axis=1)
    route = jnp.sum(hidden.astype(F32) * hidden_grad, axis=1)

    slots = rows.shape[0] // 16
    route_cols = jnp.broadcast_to(route.astype(BF)[:, None], (route.shape[0], 128))
    grad_down = down_grad(parts_y, turn(hidden))
    dx_a = dx_part(rows.reshape(4, 4, slots, -1), weights_a, shift_z)
    dx_b = dx_part(turn(rows).reshape(4, 4, slots, -1), weights_b, shift_y)
    dx_b, rows, grad_down = lax.optimization_barrier((dx_b, rows, grad_down))
    sum_a = sum_over(jnp.concatenate([dx_a, route_cols], axis=1), shift_y)
    sum_b = sum_over(dx_b, shift_z)
    grads = gate_up_grads(parts_x, rows, 0)
    sum_b, grads = lax.optimization_barrier((sum_b, grads))
    own_a = spread(sum_a, shift_z)
    own_b = spread(sum_b, shift_y)
    order = (0, 2, 3, 1)
    to_send = list(regroup([own_a[k] for k in order], [own_b[k] for k in order]))
    to_send, rows = lax.optimization_barrier((to_send, rows))
    back = to_send[:1] + [shift_x(p, -d - 1) for d, p in enumerate(to_send[1:])]
    grad_gate, grad_up = gate_up_grads(parts_x, rows, 1, grads)
    back, grad_gate, grad_up = lax.optimization_barrier((back, grad_gate, grad_up))
    swapped = swap_core(other_core(back, 1))
    scalars = jnp.concatenate([rel, jnp.stack([z, y]).astype(jnp.int32)])
    grad_tokens, grad_route = unpack(scalars, ids, route_w, table, back, swapped)
    return (
        grad_tokens,
        grad_route.T,
        grad_gate[None],
        grad_up[None],
        grad_down[None],
    )


def solution(mesh):
    both = P(("row", "col"), None)
    columns = P("col", None, "row")
    rows = P("col", "row", None)
    return jax.shard_map(
        local,
        mesh=mesh,
        in_specs=(both, both, both, both, columns, columns, rows),
        out_specs=(both, both, columns, columns, rows),
        check_vma=False,
    )
```
